32 devices in a mesh: dp: 8 (over z, x), row: 2 (over core), col: 2 (over y).
Axes of the slice: x: 2, y: 2, z: 4, core: 2. Of those that a mesh axis runs over, the one named last changes fastest.
Arguments:
- layer_input: bfloat16 [16384, 768], P(('dp', 'row', 'col')), may hold values from -6 to 6
- attn_gain: bfloat16 [768], replicated, may hold values from 0.25 to 1.75
- query_weight: bfloat16 [768, 768], P('row', 'col'), may hold values from -0.21875 to 0.21875
- key_weight: bfloat16 [768, 768], P('row', 'col'), may hold values from -0.21875 to 0.21875
- value_weight: bfloat16 [768, 768], P('row', 'col'), may hold values from -0.21875 to 0.21875
- out_weight: bfloat16 [768, 768], P('col', 'row'), may hold values from -6 to 6
- mlp_gain: bfloat16 [768], replicated, may hold values from 0.25 to 1.75
- act_weight: bfloat16 [768, 1152], P('row', 'col'), may hold values from -0.21875 to 0.21875
- lin_weight: bfloat16 [768, 1152], P('row', 'col'), may hold values from -0.21875 to 0.21875
- down_weight: bfloat16 [1152, 768], P('col', 'row'), may hold values from -0.1875 to 0.1875
- seq_lengths: int32 [8, 2], P('dp'), may hold values from 0 to 2048, as said below
- output_grad: bfloat16 [16384, 768], P(('dp', 'row', 'col')), may hold values from -6 to 6
Outputs:
- layer_output: bfloat16 [16384, 768], P(('dp', 'row', 'col'))
- grad_input: float32 [16384, 768], P(('dp', 'row', 'col'))
- grad_attn_gain: float32 [768], P(('dp', 'row', 'col'))
- grad_query: float32 [768, 768], P(('row', 'dp'), 'col')
- grad_key: float32 [768, 768], P(('row', 'dp'), 'col')
- grad_value: float32 [768, 768], P(('row', 'dp'), 'col')
- grad_out: float32 [768, 768], P('col', ('row', 'dp'))
- grad_mlp_gain: float32 [768], P(('dp', 'row', 'col'))
- grad_act: float32 [768, 1152], P(('row', 'dp'), 'col')
- grad_lin: float32 [768, 1152], P(('row', 'dp'), 'col')
- grad_down: float32 [1152, 768], P('col', ('row', 'dp'))
The draws below stay inside these ranges and needn't reach their ends.
Inputs may be any that keep to these rules, and one draw needn't show every extreme that they name: `seq_lengths`: row j holds the lengths of the sequences packed one after another from slot 0 of pack j; the nonzero lengths come first and lie between 1024 and 2048, the later ones are 0, and a row sums to at most 2048. In every draw some pack is full and holds a sequence of 2048 tokens, and some other pack holds 2 sequences of 1024 tokens.
All inputs are finite; a program needn't handle non-finite values.
Results may differ from the reference program's by a relative error of at most 0.035.
Values may be sent and summed in bfloat16 or wider, within the bound.
A program may use at most 128 MiB of HBM per device.

```python
import jax
import jax.numpy as jnp
from jax import lax

D = 768
HEADS = 12
FF = 1152
HEAD_DIM = 64
TOK_DP = 2048
LEN_LO = 1024
LEN_HI = 2048
SLOTS = 2
TOKENS = 16384
N_DP = 8


def draw_seq_lengths(key, part):
    key = jax.random.fold_in(key, 7)
    draw_key, pick_key, other_key = jax.random.split(key, 3)
    raw_lengths = jax.random.randint(draw_key, (N_DP, SLOTS), LEN_LO, LEN_HI + 1, dtype=jnp.int32)
    running = jnp.cumsum(raw_lengths, axis=1, dtype=jnp.int32)
    kept_lengths = jnp.where(running <= TOK_DP, raw_lengths, 0)
    slot_place = jnp.arange(SLOTS, dtype=jnp.int32)
    full_row = jnp.where(slot_place == 0, LEN_HI, jnp.where(slot_place < SLOTS - 1, LEN_LO, 0)).astype(jnp.int32)
    even_row = jnp.full((SLOTS,), LEN_LO, dtype=jnp.int32)
    chosen = jax.random.randint(pick_key, (), 0, N_DP, dtype=jnp.int32)
    other = (chosen + jax.random.randint(other_key, (), 1, N_DP, dtype=jnp.int32)) % N_DP
    pack_place = jnp.arange(N_DP, dtype=jnp.int32)
    with_full = jnp.where(pack_place[:, None] == chosen, full_row[None, :], kept_lengths)
    return jnp.where(pack_place[:, None] == other, even_row[None, :], with_full).astype(jnp.int32)


def with_spikes(values, own_key, source, target, parts, factor):
    def block_of(dim):
        return (jnp.arange(values.shape[dim]) // (values.shape[dim] // parts)).reshape((-1,) + (1,) * (values.ndim - 1 - dim))

    one_side = jax.random.permutation(own_key, parts)[block_of(target)]
    other_side = (block_of(target) + parts // 2) % parts
    return jnp.where((block_of(source) == one_side) | (block_of(source) == other_side), factor * values, values)


def level_of(stream_key, extent, cuts, low, high):
    loudness = 1.0
    for dim, shards_of in cuts:
        draws = jax.random.uniform(jax.random.fold_in(jax.random.fold_in(stream_key, 6), dim), (shards_of,), jnp.float32, low / len(cuts), high / len(cuts))
        loudness = loudness * jnp.repeat(jnp.exp(draws), extent[dim] // shards_of).reshape((-1,) + (1,) * (len(extent) - 1 - dim))
    return loudness


def gaussian(own_key, shape, width, bound, cuts=(), kind=jnp.bfloat16):
    values = width * jax.random.normal(own_key, shape, jnp.float32)
    if cuts:
        values = values * level_of(own_key, shape, cuts, -0.22, 0.18)
    return jnp.clip(values, -bound, bound).astype(kind)


def heavy_noise(own_key, shape, deviation, limit, pieces, heavy, kind=jnp.bfloat16):
    array = deviation * jax.random.normal(own_key, shape, jnp.float32)
    if pieces:
        array = array * level_of(own_key, shape, pieces, -0.22, 0.18)
    return jnp.clip(with_spikes(array, jax.random.fold_in(own_key, 3), *heavy), -limit, limit).astype(kind)


def setup_inputs(seed: int = 0) -> dict:
    seeds = jax.random.split(jax.random.key(seed), 13)
    return {
        "layer_input": heavy_noise(seeds[0], (TOKENS, D), 1.0, 6.0, ((0, 32),), (0, 1, 32, 2.75)),
        "attn_gain": jnp.clip(1.0 + 0.15 * jax.random.normal(seeds[1], (D,), jnp.float32), 0.25, 1.75).astype(jnp.bfloat16),
        "query_weight": gaussian(seeds[2], (D, D), D ** -0.5, 0.21875, ((0, 2), (1, 2))),
        "key_weight": gaussian(seeds[3], (D, D), D ** -0.5, 0.21875, ((0, 2), (1, 2))),
        "value_weight": gaussian(seeds[4], (D, D), D ** -0.5, 0.21875, ((0, 2), (1, 2))),
        "out_weight": gaussian(seeds[5], (D, D), (max(1, 4 * D // (3 * LEN_LO))) ** -0.5, 6.0, ((0, 2), (1, 2))),
        "mlp_gain": jnp.clip(1.0 + 0.15 * jax.random.normal(seeds[6], (D,), jnp.float32), 0.25, 1.75).astype(jnp.bfloat16),
        "act_weight": gaussian(seeds[7], (D, FF), D ** -0.5, 0.21875, ((0, 2), (1, 2))),
        "lin_weight": gaussian(seeds[8], (D, FF), D ** -0.5, 0.21875, ((0, 2), (1, 2))),
        "down_weight": gaussian(seeds[9], (FF, D), FF ** -0.5, 0.1875, ((0, 2), (1, 2))),
        "seq_lengths": draw_seq_lengths(jax.random.fold_in(seeds[12], 71), 0),
        "output_grad": heavy_noise(seeds[11], (TOKENS, D), 1.0, 6.0, ((0, 32),), (0, 1, 32, 2.75)),
    }


@jax.custom_vjp
def low(v):
    return lax.optimization_barrier(v.astype(jnp.bfloat16)).astype(jnp.float32)

@jax.custom_vjp
def low_back(v):
    return v

def low_keep(v):
    return (low(v), None)

def low_pass(kept, grad):
    return (grad,)

def back_keep(v):
    return (v, None)

def back_low(kept, grad):
    return (low(grad),)
low.defvjp(low_keep, low_pass)
low_back.defvjp(back_keep, back_low)
norm_eps = 1e-05
rope_base = 160000.0
masked_score = -1e+30
highest = lax.Precision.HIGHEST

def matmul(left_side, right_side):
    return jnp.dot(left_side, right_side, precision=highest, preferred_element_type=jnp.float32)

def halved_product(values, weight):
    split_at = values.shape[1] // 2
    first_half = low(matmul(values[:, :split_at], weight[:split_at]))
    second = low(matmul(values[:, split_at:], weight[split_at:]))
    return first_half + second

def layer_norm(stream, gain_vec):
    row_mean = lax.optimization_barrier(jnp.mean(stream, axis=1, keepdims=True))
    squares = lax.optimization_barrier(jnp.mean(stream * stream, axis=1, keepdims=True))
    normed = (stream - row_mean) * lax.rsqrt(squares - row_mean * row_mean + norm_eps)
    return low(normed * gain_vec)

def token_layout(lengths, slot_count):
    seq_ends = jnp.cumsum(lengths, dtype=jnp.int32)
    places = jnp.arange(slot_count, dtype=jnp.int32)
    passed = (places[:, None] >= seq_ends[None, :]).astype(jnp.int32)
    segment = lax.optimization_barrier(jnp.sum(passed, axis=1, dtype=jnp.int32))
    position = places - lax.optimization_barrier(jnp.sum(passed * lengths[None, :], axis=1, dtype=jnp.int32))
    return (segment, position)

def rope_tables(position, head_dim):
    half_dim = head_dim // 2
    inv_freq = rope_base ** (-2.0 * jnp.arange(half_dim, dtype=jnp.float32) / head_dim)
    angles = position.astype(jnp.float32)[:, None] * inv_freq[None, :]
    return (jnp.cos(angles), jnp.sin(angles))

def rotate(values, cos_tab, sin_tab, direction):
    row_count = values.shape[0]
    half_dim = cos_tab.shape[1]
    paired = values.reshape(row_count, -1, 2, half_dim)
    first_half = paired[:, :, 0, :]
    second_half = paired[:, :, 1, :]
    cos_part = cos_tab[:, None, :]
    sin_part = direction * sin_tab[:, None, :]
    turned = jnp.stack([first_half * cos_part - second_half * sin_part, second_half * cos_part + first_half * sin_part], axis=2)
    return turned.reshape(row_count, -1)

def attention(queries, keys_in, values_in, segment):
    row_count = queries.shape[0]
    block_rows = min(512, row_count)
    score_scale = HEAD_DIM ** (-0.5)
    query_heads = queries.reshape(row_count, HEADS, HEAD_DIM)
    key_heads = keys_in.reshape(row_count, HEADS, HEAD_DIM)
    value_heads = values_in.reshape(row_count, HEADS, HEAD_DIM)
    starts = jnp.arange(row_count // block_rows, dtype=jnp.int32) * block_rows

    def one_block(start_row):
        query_block = lax.dynamic_slice_in_dim(query_heads, start_row, block_rows, 0)
        segment_block = lax.dynamic_slice_in_dim(segment, start_row, block_rows, 0)
        scores = low_back(jnp.einsum('qhd,khd->hqk', query_block, key_heads, precision=highest) * score_scale)
        same_seq = (segment_block[:, None] == segment[None, :])[None]
        scores = jnp.where(same_seq, scores, masked_score)
        row_peak = lax.optimization_barrier(jnp.max(scores, axis=2, keepdims=True))
        exponent = jnp.exp(scores - row_peak)
        attn_probs = low(exponent / lax.optimization_barrier(jnp.sum(exponent, axis=2, keepdims=True)))
        return jnp.einsum('hqk,khd->qhd', attn_probs, value_heads, precision=highest)
    blocks = lax.map(jax.checkpoint(one_block), starts)
    return blocks.reshape(row_count, HEADS * HEAD_DIM)

def pack_forward(weight_set, pack_input, lengths):
    attn_gain, query_weight, key_weight, value_weight, out_weight, mlp_gain, act_weight, lin_weight, down_weight = weight_set
    segment, position = token_layout(lengths, pack_input.shape[0])
    cos_tab, sin_tab = rope_tables(position, HEAD_DIM)
    normed = layer_norm(pack_input, attn_gain)
    queries = low(rotate(low_back(halved_product(normed, query_weight)), cos_tab, sin_tab, 1.0))
    keys_in = low(rotate(low_back(halved_product(normed, key_weight)), cos_tab, sin_tab, 1.0))
    values_in = low(low_back(halved_product(normed, value_weight)))
    context = low(low_back(attention(queries, keys_in, values_in, segment)))
    middle = pack_input + low_back(halved_product(context, out_weight))
    normed_mlp = layer_norm(middle, mlp_gain)
    act_sum = low_back(halved_product(normed_mlp, act_weight))
    lin_sum = low_back(halved_product(normed_mlp, lin_weight))
    hidden = low(jax.nn.gelu(act_sum, approximate=False) * lin_sum)
    return middle + low_back(halved_product(hidden, down_weight))

def reference(layer_input, attn_gain, query_weight, key_weight, value_weight, out_weight, mlp_gain, act_weight, lin_weight, down_weight, seq_lengths, output_grad):
    floats = tuple((weight.astype(jnp.float32) for weight in (attn_gain, query_weight, key_weight, value_weight, out_weight, mlp_gain, act_weight, lin_weight, down_weight)))
    stream_in = layer_input.astype(jnp.float32).reshape(N_DP, TOK_DP, D)
    checked = jax.checkpoint(pack_forward)

    def forward(weight_set, stream_all):

        def one_pack(operands):
            return checked(weight_set, operands[0], operands[1])
        return lax.map(one_pack, (stream_all, seq_lengths))
    result, pull_back = jax.vjp(forward, floats, stream_in)
    weight_grads, stream_grad = pull_back(output_grad.astype(jnp.float32).reshape(N_DP, TOK_DP, D))
    return (result.reshape(TOKENS, D).astype(jnp.bfloat16), stream_grad.reshape(TOKENS, D), weight_grads[0], weight_grads[1], weight_grads[2], weight_grads[3], weight_grads[4], weight_grads[5], weight_grads[6], weight_grads[7], weight_grads[8])
```

```python
import functools

import jax
import jax.numpy as jnp
from jax import lax
from jax.experimental import pallas as pl
from jax.experimental.pallas import tpu as pltpu
from jax.sharding import PartitionSpec as P

D = 768
HEADS = 12
HEAD_DIM = 64
LANES = 128

norm_eps = 1e-05
rope_base = 160000.0
masked_score = -1e30
VMEM_BYTES = 56 * 1024 * 1024


def matmul(left_side, right_side):
    return jnp.dot(left_side, right_side, preferred_element_type=jnp.float32)


def times_transposed(left_side, right_side):
    return lax.dot_general(
        left_side, right_side, (((1,), (1,)), ((), ())), preferred_element_type=jnp.float32
    )


def transposed_times(left_side, right_side):
    return lax.dot_general(
        left_side, right_side, (((0,), (0,)), ((), ())), preferred_element_type=jnp.float32
    )


def token_layout(lengths, slot_count):
    seq_ends = jnp.cumsum(lengths, dtype=jnp.int32)
    places = jnp.arange(slot_count, dtype=jnp.int32)
    passed = (places[:, None] >= seq_ends[None, :]).astype(jnp.int32)
    segment = jnp.sum(passed, axis=1, dtype=jnp.int32)
    position = places - jnp.sum(passed * lengths[None, :], axis=1, dtype=jnp.int32)
    return (segment, position)


def norm_forward(stream, gain_vec):
    row_mean = jnp.mean(stream, axis=1, keepdims=True)
    squares = jnp.mean(stream * stream, axis=1, keepdims=True)
    inv_std = lax.rsqrt(squares - row_mean * row_mean + norm_eps)
    normed = (stream - row_mean) * inv_std
    normed_low = (normed * gain_vec.astype(jnp.float32)).astype(jnp.bfloat16)
    return (normed, inv_std, normed_low)


def norm_backward(normed_grad, normed, inv_std, gain_vec):
    scaled = normed_grad * gain_vec.astype(jnp.float32)
    first_mean = jnp.mean(scaled, axis=1, keepdims=True)
    second_mean = jnp.mean(scaled * normed, axis=1, keepdims=True)
    stream_grad = inv_std * (scaled - first_mean - normed * second_mean)
    return (stream_grad, jnp.sum(normed_grad * normed, axis=0))


def rope_lanes(position):
    half = HEAD_DIM // 2
    lane = jnp.arange(LANES, dtype=jnp.int32)
    inv_freq = rope_base ** (-2.0 * (lane % half).astype(jnp.float32) / HEAD_DIM)
    angles = position.astype(jnp.float32)[:, None] * inv_freq[None, :]
    cos_tab, sin_tab = jnp.cos(angles), jnp.sin(angles)
    low_half = (lane < half)[None, :]
    high_half = ((lane >= half) & (lane < HEAD_DIM))[None, :]
    return (cos_tab, jnp.where(low_half, -sin_tab, 0.0), jnp.where(high_half, sin_tab, 0.0))


def mask_lanes(segment):
    lane = jnp.arange(LANES, dtype=jnp.int32)[None, :]
    used = (lane >= HEAD_DIM) & (lane < HEAD_DIM + 3)
    same = (segment[:, None] + HEAD_DIM) == lane
    query_side = jnp.where(used & ~same, masked_score, 0.0)
    key_side = jnp.where(same, 1.0, 0.0)
    ones = ((lane >= HEAD_DIM + 3) & (lane < HEAD_DIM + 6)).astype(jnp.float32)
    return (query_side.astype(jnp.bfloat16), (key_side + ones).astype(jnp.bfloat16))


def turn(u, cos_tab, low_tab, high_tab):
    half = HEAD_DIM // 2
    return (
        u * cos_tab + pltpu.roll(u, LANES - half, 1) * low_tab + pltpu.roll(u, half, 1) * high_tab
    )


def forward_kernel(
    rows, h1_ref, w_ref, cos_ref, low_ref, high_ref, fq_ref, fk_ref, qa_ref, ka_ref, va_ref, ctx_ref
):
    block = pl.program_id(1)
    total = h1_ref.shape[0]

    @pl.when(block == 0)
    def _():
        def part(i, carry):
            at = pl.ds(pl.multiple_of(i * rows, rows), rows)
            u = matmul(h1_ref[at, :], w_ref[0])
            tables = (cos_ref[at, :], low_ref[at, :], high_ref[at, :])
            lane = lax.broadcasted_iota(jnp.int32, (rows, LANES), 1)
            used = lane < HEAD_DIM
            q = turn(u[:, :LANES], *tables).astype(jnp.bfloat16).astype(jnp.float32)
            k = turn(u[:, LANES : 2 * LANES], *tables)
            v = u[:, 2 * LANES :]
            scale = HEAD_DIM**-0.5
            qa_ref[0, at, :] = jnp.where(used, q * scale, fq_ref[at, :].astype(jnp.float32)).astype(
                jnp.bfloat16
            )
            ka_ref[0, at, :] = jnp.where(used, k, fk_ref[at, :].astype(jnp.float32)).astype(
                jnp.bfloat16
            )
            ones = (lane < HEAD_DIM + 3).astype(jnp.float32)
            va_ref[0, at, :] = jnp.where(used, v, ones).astype(jnp.bfloat16)
            return carry

        lax.fori_loop(0, total // rows, part, 0)

    at = pl.ds(pl.multiple_of(block * rows, rows), rows)
    scores = times_transposed(qa_ref[0, at, :], ka_ref[0])
    peak = jnp.max(scores, axis=1, keepdims=True)
    exponent = jnp.exp(scores - peak).astype(jnp.bfloat16)
    summed = matmul(exponent, va_ref[0])
    totals = summed[:, HEAD_DIM : HEAD_DIM + 1]
    lane = lax.broadcasted_iota(jnp.int32, summed.shape, 1)
    ctx_ref[0] = jnp.where(lane < HEAD_DIM, summed / totals, peak + jnp.log(totals))


def attend_forward(h1, weights, tables, feats):
    total = h1.shape[0]
    heads = weights.shape[0]
    rows = 256
    whole = lambda shape: pl.BlockSpec(shape, lambda h, i: (0,) * len(shape))
    per_head = lambda shape: pl.BlockSpec((1, *shape), lambda h, i: (h, 0, 0))
    out = jax.ShapeDtypeStruct((heads, total, LANES), jnp.bfloat16)
    return pl.pallas_call(
        functools.partial(forward_kernel, rows),
        grid=(heads, total // rows),
        in_specs=[whole(h1.shape), per_head(weights.shape[1:])] + [whole((total, LANES))] * 5,
        out_specs=[per_head((total, LANES))] * 3
        + [pl.BlockSpec((1, rows, LANES), lambda h, i: (h, i, 0))],
        out_shape=[out, out, out, jax.ShapeDtypeStruct((heads, total, LANES), jnp.float32)],
        compiler_params=pltpu.CompilerParams(
            vmem_limit_bytes=VMEM_BYTES, dimension_semantics=("arbitrary", "arbitrary")
        ),
        cost_estimate=pl.CostEstimate(
            flops=heads * total * total * 1024, bytes_accessed=1 << 24, transcendentals=0
        ),
        name="attend_forward",
    )(h1, weights, *tables, *feats)


def backward_kernel(
    rows, qa_ref, ka_ref, va_ref, ga_ref, cos_ref, low_ref, high_ref, out_ref, dk_acc, dv_acc
):
    block = pl.program_id(1)
    last = pl.num_programs(1) - 1
    total = ka_ref.shape[1]
    at = pl.ds(pl.multiple_of(block * rows, rows), rows)
    qa = qa_ref[0, at, :]
    ga = ga_ref[0, at, :]
    probs = jnp.exp(times_transposed(ka_ref[0], qa))
    probs_low = probs.astype(jnp.bfloat16)
    dprobs = times_transposed(va_ref[0], ga)
    dscores = (probs * dprobs).astype(jnp.bfloat16)
    dv = matmul(probs_low, ga)
    dk = matmul(dscores, qa)

    @pl.when(block == 0)
    def _():
        dv_acc[...] = dv
        dk_acc[...] = dk

    @pl.when(block > 0)
    def _():
        dv_acc[...] += dv
        dk_acc[...] += dk

    dq = transposed_times(dscores, ka_ref[0]) * HEAD_DIM**-0.5
    used = lax.broadcasted_iota(jnp.int32, (rows, LANES), 1) < HEAD_DIM

    def back(u, at):
        u = jnp.where(used, u, 0.0)
        return jnp.where(used, turn(u, cos_ref[at, :], -low_ref[at, :], -high_ref[at, :]), 0.0)

    out_ref[0, at, :LANES] = back(dq, at).astype(jnp.bfloat16)

    @pl.when(block == last)
    def _():
        def part(i, carry):
            here = pl.ds(pl.multiple_of(i * rows, rows), rows)
            out_ref[0, here, LANES : 2 * LANES] = back(dk_acc[here, :], here).astype(jnp.bfloat16)
            out_ref[0, here, 2 * LANES :] = jnp.where(used, dv_acc[here, :], 0.0).astype(
                jnp.bfloat16
            )
            return carry

        lax.fori_loop(0, total // rows, part, 0)


def attend_backward(qa, ka, va, ga, tables):
    heads, total, _ = qa.shape
    rows = 256
    whole = lambda shape: pl.BlockSpec(shape, lambda h, i: (0,) * len(shape))
    per_head = lambda shape: pl.BlockSpec((1, *shape), lambda h, i: (h, 0, 0))
    return pl.pallas_call(
        functools.partial(backward_kernel, rows),
        grid=(heads, total // rows),
        in_specs=[per_head((total, LANES))] * 4 + [whole((total, LANES))] * 3,
        out_specs=per_head((total, 3 * LANES)),
        out_shape=jax.ShapeDtypeStruct((heads, total, 3 * LANES), jnp.bfloat16),
        scratch_shapes=[pltpu.VMEM((total, LANES), jnp.float32)] * 2,
        compiler_params=pltpu.CompilerParams(
            vmem_limit_bytes=VMEM_BYTES, dimension_semantics=("arbitrary", "arbitrary")
        ),
        cost_estimate=pl.CostEstimate(
            flops=heads * total * total * 2560, bytes_accessed=1 << 24, transcendentals=0
        ),
        name="attend_backward",
    )(qa, ka, va, ga, *tables)


def three_parts(values):
    high = values.astype(jnp.bfloat16)
    rest = values - high.astype(jnp.float32)
    middle = rest.astype(jnp.bfloat16)
    low = (rest - middle.astype(jnp.float32)).astype(jnp.bfloat16)
    return jnp.concatenate([high, middle, low], axis=-1)


def swap_tokens_for_heads(values):
    quarter = values.shape[0]
    cut = values.reshape(quarter, 2, 2, -1).transpose(2, 1, 0, 3).reshape(4, quarter, -1)
    return lax.all_to_all(cut, ("row", "col"), split_axis=0, concat_axis=0, tiled=True).reshape(
        4 * quarter, -1
    )


def swap_heads_for_tokens(values):
    quarter = values.shape[0] // 4
    got = lax.all_to_all(
        values.reshape(4, quarter, -1), ("row", "col"), split_axis=0, concat_axis=0, tiled=True
    )
    return got.reshape(2, 2, quarter, -1).transpose(2, 1, 0, 3).reshape(quarter, -1)


def gather_quarters(values):
    return lax.all_gather(values, ("row", "col"), axis=0, tiled=True)


def whole_weight(weight, first, second):
    weight = lax.all_gather(weight, second, axis=1, tiled=True)
    return lax.all_gather(weight, first, axis=0, tiled=True)


def sum_over_packs(array, dim):
    parts = lax.axis_size("dp")
    shape = array.shape
    cut = array.reshape(*shape[:dim], parts, shape[dim] // parts, *shape[dim + 1 :])
    cut = jnp.moveaxis(cut, dim, 0)
    arrived = lax.all_to_all(cut, "dp", split_axis=0, concat_axis=0, tiled=True)
    return arrived.astype(jnp.float32).sum(axis=0)


def shards(
    layer_input,
    attn_gain,
    query_weight,
    key_weight,
    value_weight,
    out_weight,
    mlp_gain,
    act_weight,
    lin_weight,
    down_weight,
    seq_lengths,
    output_grad,
):
    bf16 = jnp.bfloat16
    stream = layer_input.astype(jnp.float32)
    quarter = stream.shape[0]
    total = quarter * 4
    segment, position = token_layout(seq_lengths[0], total)
    tables = rope_lanes(position)
    feats = mask_lanes(segment)
    normed_attn, inv_attn, low_attn = norm_forward(stream, attn_gain)

    stacked = jnp.stack((query_weight, key_weight, value_weight), axis=1)
    own = lax.all_to_all(stacked, "row", split_axis=2, concat_axis=0, tiled=True)
    own_heads = own.shape[2] // HEAD_DIM
    per_head = own.reshape(D, 3, own_heads, HEAD_DIM).transpose(2, 0, 1, 3)
    head_weights = jnp.pad(per_head, ((0, 0), (0, 0), (0, 0), (0, LANES - HEAD_DIM))).reshape(
        own_heads, D, 3 * LANES
    )

    h1 = gather_quarters(low_attn)
    qa, ka, va, ctx = attend_forward(h1, head_weights, tables, feats)
    context_heads = ctx[:, :, :HEAD_DIM]
    context_own = context_heads.astype(bf16).transpose(1, 0, 2).reshape(total, -1)

    out_whole = whole_weight(out_weight, "col", "row")
    act_whole = whole_weight(act_weight, "row", "col")
    lin_whole = whole_weight(lin_weight, "row", "col")
    down_whole = whole_weight(down_weight, "col", "row")

    context = swap_heads_for_tokens(context_own)
    middle = stream + matmul(context, out_whole)
    normed_mlp, inv_mlp, low_mlp = norm_forward(middle, mlp_gain)
    act = matmul(low_mlp, act_whole)
    lin = matmul(low_mlp, lin_whole)
    cdf = 0.5 * (1.0 + lax.erf(act * (0.5**0.5)))
    gelu = act * cdf
    hidden = (gelu * lin).astype(bf16)
    layer_output = (middle + matmul(hidden, down_whole)).astype(bf16)

    top_grad = output_grad.astype(jnp.float32)
    grad_down = transposed_times(hidden, output_grad).astype(bf16)
    hidden_grad = times_transposed(output_grad, down_whole)
    pdf = jnp.exp(-0.5 * act * act) * (0.5 / jnp.pi) ** 0.5
    act_grad = (hidden_grad * lin * (cdf + act * pdf)).astype(bf16)
    lin_grad = (hidden_grad * gelu).astype(bf16)
    grad_act = transposed_times(low_mlp, act_grad).astype(bf16)
    grad_lin = transposed_times(low_mlp, lin_grad).astype(bf16)
    mlp_norm_grad = times_transposed(act_grad, act_whole) + times_transposed(lin_grad, lin_whole)
    middle_back, gain_mlp_part = norm_backward(mlp_norm_grad, normed_mlp, inv_mlp, mlp_gain)
    middle_grad = top_grad + middle_back
    attn_grad = middle_grad.astype(bf16)
    grad_out = transposed_times(context, attn_grad).astype(bf16)
    context_grad = times_transposed(attn_grad, out_whole).astype(bf16)
    grad_own = swap_tokens_for_heads(context_grad)

    grad_heads = grad_own.reshape(total, own_heads, HEAD_DIM).transpose(1, 0, 2)
    inner = jnp.sum(grad_heads.astype(jnp.float32) * context_heads, axis=2, keepdims=True)
    ga = jnp.pad(
        jnp.concatenate([grad_heads, three_parts(-inner)], axis=2),
        ((0, 0), (0, 0), (0, LANES - HEAD_DIM - 3)),
    )
    minus_total = three_parts(-ctx[:, :, HEAD_DIM : HEAD_DIM + 1])
    qa = jnp.concatenate(
        [qa[:, :, : HEAD_DIM + 3], minus_total, qa[:, :, HEAD_DIM + 6 :]], axis=2
    )
    qkv_grad = attend_backward(qa, ka, va, ga, tables)

    norm_partial = lax.dot_general(
        qkv_grad,
        head_weights,
        (((0, 2), (0, 2)), ((), ())),
        preferred_element_type=jnp.float32,
    ).astype(bf16)
    pieces = lax.all_to_all(
        norm_partial.reshape(4, quarter, D), ("row", "col"), split_axis=0, concat_axis=0, tiled=True
    )
    attn_norm_grad = pieces.astype(jnp.float32).sum(axis=0)
    head_grads = lax.dot_general(
        h1, qkv_grad, (((0,), (1,)), ((), ())), preferred_element_type=jnp.float32
    ).astype(bf16)
    head_grads = head_grads.reshape(D, own_heads, 3, LANES)[..., :HEAD_DIM]
    head_grads = head_grads.transpose(0, 2, 1, 3).reshape(D, 3, own_heads * HEAD_DIM)
    attn_weight_grad = lax.all_to_all(head_grads, "row", split_axis=0, concat_axis=2, tiled=True)
    stream_back, gain_attn_part = norm_backward(attn_norm_grad, normed_attn, inv_attn, attn_gain)
    grad_input = middle_grad + stream_back

    def over_group(array, first, second):
        array = lax.psum_scatter(array, first, scatter_dimension=0, tiled=True)
        return lax.psum_scatter(array, second, scatter_dimension=1, tiled=True)

    grad_out = sum_over_packs(over_group(grad_out, "col", "row"), 1)
    grad_down = sum_over_packs(over_group(grad_down, "col", "row"), 1)
    grad_act = sum_over_packs(over_group(grad_act, "row", "col"), 0)
    grad_lin = sum_over_packs(over_group(grad_lin, "row", "col"), 0)
    qkv_sums = sum_over_packs(attn_weight_grad, 0)
    gains = lax.psum_scatter(
        jnp.stack((gain_attn_part, gain_mlp_part), axis=1),
        ("dp", "row", "col"),
        scatter_dimension=0,
        tiled=True,
    )
    return (
        layer_output,
        grad_input,
        gains[:, 0],
        qkv_sums[:, 0],
        qkv_sums[:, 1],
        qkv_sums[:, 2],
        grad_out,
        gains[:, 1],
        grad_act,
        grad_lin,
        grad_down,
    )


def solution(mesh):
    in_specs = (
        P(("dp", "row", "col"), None),
        P(),
        P("row", "col"),
        P("row", "col"),
        P("row", "col"),
        P("col", "row"),
        P(),
        P("row", "col"),
        P("row", "col"),
        P("col", "row"),
        P("dp", None),
        P(("dp", "row", "col"), None),
    )
    out_specs = (
        P(("dp", "row", "col"), None),
        P(("dp", "row", "col"), None),
        P(("dp", "row", "col")),
        P(("row", "dp"), "col"),
        P(("row", "dp"), "col"),
        P(("row", "dp"), "col"),
        P("col", ("row", "dp")),
        P(("dp", "row", "col")),
        P(("row", "dp"), "col"),
        P(("row", "dp"), "col"),
        P("col", ("row", "dp")),
    )
    return jax.shard_map(shards, mesh=mesh, in_specs=in_specs, out_specs=out_specs, check_vma=False)
```

```python
import functools

import jax
import jax.numpy as jnp
from jax import lax
from jax.experimental import pallas as pl
from jax.experimental.pallas import tpu as pltpu
from jax.sharding import PartitionSpec as P

D = 768
HEADS = 12
HEAD_DIM = 64
LANES = 128

norm_eps = 1e-05
rope_base = 160000.0
masked_score = -1e30
VMEM_BYTES = 56 * 1024 * 1024


def matmul(left_side, right_side):
    return jnp.dot(left_side, right_side, preferred_element_type=jnp.float32)


def times_transposed(left_side, right_side):
    return lax.dot_general(
        left_side, right_side, (((1,), (1,)), ((), ())), preferred_element_type=jnp.float32
    )


def transposed_times(left_side, right_side):
    return lax.dot_general(
        left_side, right_side, (((0,), (0,)), ((), ())), preferred_element_type=jnp.float32
    )


def token_layout(lengths, slot_count):
    seq_ends = jnp.cumsum(lengths, dtype=jnp.int32)
    places = jnp.arange(slot_count, dtype=jnp.int32)
    passed = (places[:, None] >= seq_ends[None, :]).astype(jnp.int32)
    segment = jnp.sum(passed, axis=1, dtype=jnp.int32)
    position = places - jnp.sum(passed * lengths[None, :], axis=1, dtype=jnp.int32)
    return (segment, position)


def norm_forward(stream, gain_vec):
    row_mean = jnp.mean(stream, axis=1, keepdims=True)
    squares = jnp.mean(stream * stream, axis=1, keepdims=True)
    inv_std = lax.rsqrt(squares - row_mean * row_mean + norm_eps)
    normed = (stream - row_mean) * inv_std
    normed_low = (normed * gain_vec.astype(jnp.float32)).astype(jnp.bfloat16)
    return (normed, inv_std, normed_low)


def norm_backward(normed_grad, normed, inv_std, gain_vec):
    scaled = normed_grad * gain_vec.astype(jnp.float32)
    first_mean = jnp.mean(scaled, axis=1, keepdims=True)
    second_mean = jnp.mean(scaled * normed, axis=1, keepdims=True)
    stream_grad = inv_std * (scaled - first_mean - normed * second_mean)
    return (stream_grad, jnp.sum(normed_grad * normed, axis=0))


def rope_lanes(position):
    half = HEAD_DIM // 2
    lane = jnp.arange(LANES, dtype=jnp.int32)
    inv_freq = rope_base ** (-2.0 * (lane % half).astype(jnp.float32) / HEAD_DIM)
    angles = position.astype(jnp.float32)[:, None] * inv_freq[None, :]
    cos_tab, sin_tab = jnp.cos(angles), jnp.sin(angles)
    low_half = (lane < half)[None, :]
    high_half = ((lane >= half) & (lane < HEAD_DIM))[None, :]
    return (cos_tab, jnp.where(low_half, -sin_tab, 0.0), jnp.where(high_half, sin_tab, 0.0))


def mask_lanes(segment):
    lane = jnp.arange(LANES, dtype=jnp.int32)[None, :]
    used = (lane >= HEAD_DIM) & (lane < HEAD_DIM + 3)
    same = (segment[:, None] + HEAD_DIM) == lane
    query_side = jnp.where(used & ~same, masked_score, 0.0)
    key_side = jnp.where(same, 1.0, 0.0)
    ones = ((lane >= HEAD_DIM + 3) & (lane < HEAD_DIM + 6)).astype(jnp.float32)
    return (query_side.astype(jnp.bfloat16), (key_side + ones).astype(jnp.bfloat16))


def turn(u, cos_tab, low_tab, high_tab):
    half = HEAD_DIM // 2
    return (
        u * cos_tab + pltpu.roll(u, LANES - half, 1) * low_tab + pltpu.roll(u, half, 1) * high_tab
    )


def forward_kernel(
    rows, h1_ref, w_ref, cos_ref, low_ref, high_ref, fq_ref, fk_ref, qa_ref, ka_ref, va_ref, ctx_ref
):
    block = pl.program_id(1)
    total = h1_ref.shape[0]

    @pl.when(block == 0)
    def _():
        def part(i, carry):
            at = pl.ds(pl.multiple_of(i * rows, rows), rows)
            u = matmul(h1_ref[at, :], w_ref[0])
            tables = (cos_ref[at, :], low_ref[at, :], high_ref[at, :])
            lane = lax.broadcasted_iota(jnp.int32, (rows, LANES), 1)
            used = lane < HEAD_DIM
            q = turn(u[:, :LANES], *tables).astype(jnp.bfloat16).astype(jnp.float32)
            k = turn(u[:, LANES : 2 * LANES], *tables)
            v = u[:, 2 * LANES :]
            scale = HEAD_DIM**-0.5
            qa_ref[0, at, :] = jnp.where(used, q * scale, fq_ref[at, :].astype(jnp.float32)).astype(
                jnp.bfloat16
            )
            ka_ref[0, at, :] = jnp.where(used, k, fk_ref[at, :].astype(jnp.float32)).astype(
                jnp.bfloat16
            )
            ones = (lane < HEAD_DIM + 3).astype(jnp.float32)
            va_ref[0, at, :] = jnp.where(used, v, ones).astype(jnp.bfloat16)
            return carry

        lax.fori_loop(0, total // rows, part, 0)

    at = pl.ds(pl.multiple_of(block * rows, rows), rows)
    scores = times_transposed(qa_ref[0, at, :], ka_ref[0])
    peak = jnp.max(scores, axis=1, keepdims=True)
    exponent = jnp.exp(scores - peak).astype(jnp.bfloat16)
    summed = matmul(exponent, va_ref[0])
    totals = summed[:, HEAD_DIM : HEAD_DIM + 1]
    lane = lax.broadcasted_iota(jnp.int32, summed.shape, 1)
    ctx_ref[0] = jnp.where(lane < HEAD_DIM, summed / totals, peak + jnp.log(totals))


def attend_forward(h1, weights, tables, feats):
    total = h1.shape[0]
    heads = weights.shape[0]
    rows = 256
    whole = lambda shape: pl.BlockSpec(shape, lambda h, i: (0,) * len(shape))
    per_head = lambda shape: pl.BlockSpec((1, *shape), lambda h, i: (h, 0, 0))
    out = jax.ShapeDtypeStruct((heads, total, LANES), jnp.bfloat16)
    return pl.pallas_call(
        functools.partial(forward_kernel, rows),
        grid=(heads, total // rows),
        in_specs=[whole(h1.shape), per_head(weights.shape[1:])] + [whole((total, LANES))] * 5,
        out_specs=[per_head((total, LANES))] * 3
        + [pl.BlockSpec((1, rows, LANES), lambda h, i: (h, i, 0))],
        out_shape=[out, out, out, jax.ShapeDtypeStruct((heads, total, LANES), jnp.float32)],
        compiler_params=pltpu.CompilerParams(
            vmem_limit_bytes=VMEM_BYTES, dimension_semantics=("arbitrary", "arbitrary")
        ),
        cost_estimate=pl.CostEstimate(
            flops=heads * total * total * 1024, bytes_accessed=1 << 24, transcendentals=0
        ),
        name="attend_forward",
    )(h1, weights, *tables, *feats)


def backward_kernel(
    rows,
    qa_ref,
    ka_ref,
    va_ref,
    g_ref,
    ctx_ref,
    cos_ref,
    low_ref,
    high_ref,
    out_ref,
    qa_full,
    ga_full,
    dk_acc,
    dv_acc,
):
    block = pl.program_id(1)
    last = pl.num_programs(1) - 1
    total = ka_ref.shape[1]
    lane = lax.broadcasted_iota(jnp.int32, (rows, LANES), 1)
    used = lane < HEAD_DIM

    def with_parts(base, first, column):
        high = column.astype(jnp.bfloat16).astype(jnp.float32)
        middle = (column - high).astype(jnp.bfloat16).astype(jnp.float32)
        base = jnp.where(lane == first, high, base)
        base = jnp.where(lane == first + 1, middle, base)
        return jnp.where(lane == first + 2, column - high - middle, base).astype(jnp.bfloat16)

    @pl.when(block == 0)
    def _():
        def part(i, carry):
            here = pl.ds(pl.multiple_of(i * rows, rows), rows)
            g = g_ref[0, here, :].astype(jnp.float32)
            g = jnp.concatenate([g, jnp.zeros_like(g)], axis=1)
            ctx = ctx_ref[0, here, :]
            inner = jnp.sum(jnp.where(used, g * ctx, 0.0), axis=1, keepdims=True)
            ga_full[here, :] = with_parts(g, HEAD_DIM, -inner)
            qa_full[here, :] = with_parts(
                qa_ref[0, here, :].astype(jnp.float32),
                HEAD_DIM + 3,
                -ctx[:, HEAD_DIM : HEAD_DIM + 1],
            )
            return carry

        lax.fori_loop(0, total // rows, part, 0)

    at = pl.ds(pl.multiple_of(block * rows, rows), rows)
    qa = qa_full[at, :]
    ga = ga_full[at, :]
    probs = jnp.exp(times_transposed(ka_ref[0], qa))
    probs_low = probs.astype(jnp.bfloat16)
    dprobs = times_transposed(va_ref[0], ga)
    dscores = (probs * dprobs).astype(jnp.bfloat16)
    dv = matmul(probs_low, ga)
    dk = matmul(dscores, qa)

    @pl.when(block == 0)
    def _():
        dv_acc[...] = dv
        dk_acc[...] = dk

    @pl.when(block > 0)
    def _():
        dv_acc[...] += dv
        dk_acc[...] += dk

    dq = transposed_times(dscores, ka_ref[0]) * HEAD_DIM**-0.5

    def back(u, at):
        u = jnp.where(used, u, 0.0)
        return jnp.where(used, turn(u, cos_ref[at, :], -low_ref[at, :], -high_ref[at, :]), 0.0)

    out_ref[0, at, :LANES] = back(dq, at).astype(jnp.bfloat16)

    @pl.when(block == last)
    def _():
        def part(i, carry):
            here = pl.ds(pl.multiple_of(i * rows, rows), rows)
            out_ref[0, here, LANES : 2 * LANES] = back(dk_acc[here, :], here).astype(jnp.bfloat16)
            out_ref[0, here, 2 * LANES :] = jnp.where(used, dv_acc[here, :], 0.0).astype(
                jnp.bfloat16
            )
            return carry

        lax.fori_loop(0, total // rows, part, 0)


def attend_backward(qa, ka, va, grads, ctx, tables):
    heads, total, _ = qa.shape
    rows = 256
    whole = lambda shape: pl.BlockSpec(shape, lambda h, i: (0,) * len(shape))
    per_head = lambda shape: pl.BlockSpec((1, *shape), lambda h, i: (h, 0, 0))
    return pl.pallas_call(
        functools.partial(backward_kernel, rows),
        grid=(heads, total // rows),
        in_specs=[per_head((total, LANES))] * 3
        + [per_head((total, HEAD_DIM)), per_head((total, LANES))]
        + [whole((total, LANES))] * 3,
        out_specs=per_head((total, 3 * LANES)),
        out_shape=jax.ShapeDtypeStruct((heads, total, 3 * LANES), jnp.bfloat16),
        scratch_shapes=[pltpu.VMEM((total, LANES), jnp.bfloat16)] * 2
        + [pltpu.VMEM((total, LANES), jnp.float32)] * 2,
        compiler_params=pltpu.CompilerParams(
            vmem_limit_bytes=VMEM_BYTES, dimension_semantics=("arbitrary", "arbitrary")
        ),
        cost_estimate=pl.CostEstimate(
            flops=heads * total * total * 2560, bytes_accessed=1 << 24, transcendentals=0
        ),
        name="attend_backward",
    )(qa, ka, va, grads, ctx, *tables)


def pack_sum_kernel(peers, x_ref, out_ref, got, send_sems, recv_sems):
    me = lax.axis_index("dp")
    barrier = pltpu.get_barrier_semaphore()
    for d in range(1, peers):
        pl.semaphore_signal(
            barrier,
            inc=1,
            device_id={"dp": lax.rem(me + d, peers)},
            device_id_type=pl.DeviceIdType.MESH,
        )
    pl.semaphore_wait(barrier, peers - 1)
    copies = []
    for d in range(1, peers):
        peer = lax.rem(me + d, peers)
        copy = pltpu.make_async_remote_copy(
            src_ref=x_ref.at[peer],
            dst_ref=got.at[d - 1],
            send_sem=send_sems.at[d - 1],
            recv_sem=recv_sems.at[d - 1],
            device_id={"dp": peer},
            device_id_type=pl.DeviceIdType.MESH,
        )
        copy.start()
        copies.append(copy)
    out_ref[...] = x_ref[me].astype(jnp.float32)
    for d, copy in enumerate(copies):
        copy.wait_recv()
        out_ref[...] += got[d].astype(jnp.float32)
    for copy in copies:
        copy.wait_send()


def sum_over_packs(array, collective_id):
    peers = array.shape[0]
    vmem = pl.BlockSpec(memory_space=pltpu.VMEM)
    return pl.pallas_call(
        functools.partial(pack_sum_kernel, peers),
        in_specs=[vmem],
        out_specs=vmem,
        out_shape=jax.ShapeDtypeStruct(array.shape[1:], jnp.float32),
        scratch_shapes=[
            pltpu.VMEM((peers - 1, *array.shape[1:]), jnp.bfloat16),
            pltpu.SemaphoreType.DMA((peers - 1,)),
            pltpu.SemaphoreType.DMA((peers - 1,)),
        ],
        compiler_params=pltpu.CompilerParams(
            vmem_limit_bytes=VMEM_BYTES, collective_id=collective_id, has_side_effects=True
        ),
        name="sum_over_packs",
    )(array)


def swapped(array, axis):
    return lax.ppermute(array, axis, [(0, 1), (1, 0)])


def kept_and_sent(halves, axis):
    me = lax.axis_index(axis)
    sent = lax.dynamic_index_in_dim(halves, 1 - me, 0, keepdims=False)
    kept = lax.dynamic_index_in_dim(halves, me, 0, keepdims=False)
    other = swapped(sent, axis)
    return (kept.astype(jnp.float32) + other.astype(jnp.float32)).astype(jnp.bfloat16)


def swap_tokens_for_heads(values):
    quarter = values.shape[0]
    cut = values.reshape(quarter, 2, 2, -1).transpose(2, 1, 0, 3).reshape(4, quarter, -1)
    return lax.all_to_all(cut, ("row", "col"), split_axis=0, concat_axis=0, tiled=True).reshape(
        4 * quarter, -1
    )


def swap_heads_for_tokens(values):
    quarter = values.shape[0] // 4
    got = lax.all_to_all(
        values.reshape(4, quarter, -1), ("row", "col"), split_axis=0, concat_axis=0, tiled=True
    )
    return got.reshape(2, 2, quarter, -1).transpose(2, 1, 0, 3).reshape(quarter, -1)


def gather_quarters(values):
    return lax.all_gather(values, ("row", "col"), axis=0, tiled=True)


def whole_weight(weight, first, second):
    weight = lax.all_gather(weight, second, axis=1, tiled=True)
    return lax.all_gather(weight, first, axis=0, tiled=True)


def shards(
    layer_input,
    attn_gain,
    query_weight,
    key_weight,
    value_weight,
    out_weight,
    mlp_gain,
    act_weight,
    lin_weight,
    down_weight,
    seq_lengths,
    output_grad,
):
    bf16 = jnp.bfloat16
    stream = layer_input.astype(jnp.float32)
    quarter = stream.shape[0]
    total = quarter * 4
    segment, position = token_layout(seq_lengths[0], total)
    tables = rope_lanes(position)
    feats = mask_lanes(segment)
    normed_attn, inv_attn, low_attn = norm_forward(stream, attn_gain)

    stacked = jnp.stack((query_weight, key_weight, value_weight), axis=1)
    own = lax.all_to_all(stacked, "row", split_axis=2, concat_axis=0, tiled=True)
    own_heads = own.shape[2] // HEAD_DIM
    per_head = own.reshape(D, 3, own_heads, HEAD_DIM).transpose(2, 0, 1, 3)
    head_weights = jnp.pad(per_head, ((0, 0), (0, 0), (0, 0), (0, LANES - HEAD_DIM))).reshape(
        own_heads, D, 3 * LANES
    )

    h1 = gather_quarters(low_attn)
    qa, ka, va, ctx = attend_forward(h1, head_weights, tables, feats)
    context_heads = ctx[:, :, :HEAD_DIM]
    context_own = context_heads.astype(bf16).transpose(1, 0, 2).reshape(total, -1)

    out_whole = whole_weight(out_weight, "col", "row")
    act_whole = whole_weight(act_weight, "row", "col")
    lin_whole = whole_weight(lin_weight, "row", "col")
    down_whole = whole_weight(down_weight, "col", "row")

    context = swap_heads_for_tokens(context_own)
    middle = stream + matmul(context, out_whole)
    normed_mlp, inv_mlp, low_mlp = norm_forward(middle, mlp_gain)
    act = matmul(low_mlp, act_whole)
    lin = matmul(low_mlp, lin_whole)
    cdf = 0.5 * (1.0 + lax.erf(act * (0.5**0.5)))
    gelu = act * cdf
    hidden = (gelu * lin).astype(bf16)
    layer_output = (middle + matmul(hidden, down_whole)).astype(bf16)

    top_grad = output_grad.astype(jnp.float32)
    grad_down = transposed_times(output_grad, hidden).astype(bf16)
    hidden_grad = times_transposed(output_grad, down_whole)
    pdf = jnp.exp(-0.5 * act * act) * (0.5 / jnp.pi) ** 0.5
    act_grad = (hidden_grad * lin * (cdf + act * pdf)).astype(bf16)
    lin_grad = (hidden_grad * gelu).astype(bf16)
    grad_act = transposed_times(low_mlp, act_grad).astype(bf16)
    grad_lin = transposed_times(low_mlp, lin_grad).astype(bf16)
    mlp_norm_grad = times_transposed(act_grad, act_whole) + times_transposed(lin_grad, lin_whole)
    middle_back, gain_mlp_part = norm_backward(mlp_norm_grad, normed_mlp, inv_mlp, mlp_gain)
    middle_grad = top_grad + middle_back
    attn_grad = middle_grad.astype(bf16)
    grad_out = transposed_times(attn_grad, context).astype(bf16)
    half = D // 2
    by_col = [
        jnp.concatenate(
            [g[:, c * (g.shape[1] // 2) : (c + 1) * (g.shape[1] // 2)] for g in grads], axis=1
        )
        for grads in [(grad_act, grad_lin, grad_down, grad_out)]
        for c in range(2)
    ]
    stacked_grads = jnp.stack(by_col, axis=0).reshape(2, 2, half, -1).swapaxes(0, 1)
    group_grads = kept_and_sent(kept_and_sent(stacked_grads, "row"), "col")
    context_grad = times_transposed(attn_grad, out_whole).astype(bf16)
    grad_own = swap_tokens_for_heads(context_grad)

    grad_heads = grad_own.reshape(total, own_heads, HEAD_DIM).transpose(1, 0, 2)
    qkv_grad = attend_backward(qa, ka, va, grad_heads, ctx, tables)

    norm_partial = lax.dot_general(
        qkv_grad,
        head_weights,
        (((0, 2), (0, 2)), ((), ())),
        preferred_element_type=jnp.float32,
    ).astype(bf16)
    pieces = lax.all_to_all(
        norm_partial.reshape(4, quarter, D), ("row", "col"), split_axis=0, concat_axis=0, tiled=True
    )
    attn_norm_grad = pieces.astype(jnp.float32).sum(axis=0)
    head_grads = lax.dot_general(
        h1, qkv_grad, (((0,), (1,)), ((), ())), preferred_element_type=jnp.float32
    ).astype(bf16)
    head_grads = head_grads.reshape(D, own_heads, 3, LANES)[..., :HEAD_DIM]
    head_grads = head_grads.transpose(0, 2, 1, 3).reshape(D, 3, own_heads * HEAD_DIM)
    attn_weight_grad = lax.all_to_all(head_grads, "row", split_axis=0, concat_axis=2, tiled=True)
    stream_back, gain_attn_part = norm_backward(attn_norm_grad, normed_attn, inv_attn, attn_gain)
    grad_input = middle_grad + stream_back

    peers = lax.axis_size("dp")
    mine = jnp.concatenate([attn_weight_grad.reshape(half, -1), group_grads], axis=1)
    summed = sum_over_packs(mine.reshape(peers, half // peers, -1), 0)
    wide = 3 * half
    qkv_sums = summed[:, :wide].reshape(-1, 3, half)
    ff = act_weight.shape[1]
    grad_act, grad_lin, grad_down = (
        summed[:, wide + i * ff : wide + (i + 1) * ff] for i in range(3)
    )
    grad_out = summed[:, wide + 3 * ff :].T
    grad_down = grad_down.T
    devices = peers * 4
    gain_parts = jnp.stack((gain_attn_part, gain_mlp_part), axis=0).reshape(2, devices, -1)
    gains = (
        lax.all_to_all(
            gain_parts.swapaxes(0, 1).reshape(devices, -1),
            ("dp", "row", "col"),
            split_axis=0,
            concat_axis=0,
            tiled=True,
        )
        .sum(axis=0)
        .reshape(2, -1)
    )
    return (
        layer_output,
        grad_input,
        gains[0],
        qkv_sums[:, 0],
        qkv_sums[:, 1],
        qkv_sums[:, 2],
        grad_out,
        gains[1],
        grad_act,
        grad_lin,
        grad_down,
    )


def solution(mesh):
    in_specs = (
        P(("dp", "row", "col"), None),
        P(),
        P("row", "col"),
        P("row", "col"),
        P("row", "col"),
        P("col", "row"),
        P(),
        P("row", "col"),
        P("row", "col"),
        P("col", "row"),
        P("dp", None),
        P(("dp", "row", "col"), None),
    )
    out_specs = (
        P(("dp", "row", "col"), None),
        P(("dp", "row", "col"), None),
        P(("dp", "row", "col")),
        P(("row", "dp"), "col"),
        P(("row", "dp"), "col"),
        P(("row", "dp"), "col"),
        P("col", ("row", "dp")),
        P(("dp", "row", "col")),
        P(("row", "dp"), "col"),
        P(("row", "dp"), "col"),
        P("col", ("row", "dp")),
    )
    return jax.shard_map(shards, mesh=mesh, in_specs=in_specs, out_specs=out_specs, check_vma=False)
```

```python
import functools

import jax
import jax.numpy as jnp
from jax import lax
from jax.experimental import pallas as pl
from jax.experimental.pallas import tpu as pltpu
from jax.sharding import PartitionSpec as P

D = 768
HEADS = 12
HEAD_DIM = 64
LANES = 128

norm_eps = 1e-05
rope_base = 160000.0
masked_score = -1e30
VMEM_BYTES = 56 * 1024 * 1024


def matmul(left_side, right_side):
    return jnp.dot(left_side, right_side, preferred_element_type=jnp.float32)


def times_transposed(left_side, right_side):
    return lax.dot_general(
        left_side, right_side, (((1,), (1,)), ((), ())), preferred_element_type=jnp.float32
    )


def transposed_times(left_side, right_side):
    return lax.dot_general(
        left_side, right_side, (((0,), (0,)), ((), ())), preferred_element_type=jnp.float32
    )


def token_layout(lengths, slot_count):
    seq_ends = jnp.cumsum(lengths, dtype=jnp.int32)
    places = jnp.arange(slot_count, dtype=jnp.int32)
    passed = (places[:, None] >= seq_ends[None, :]).astype(jnp.int32)
    segment = jnp.sum(passed, axis=1, dtype=jnp.int32)
    position = places - jnp.sum(passed * lengths[None, :], axis=1, dtype=jnp.int32)
    return (segment, position)


def norm_forward(stream, gain_vec):
    row_mean = jnp.mean(stream, axis=1, keepdims=True)
    squares = jnp.mean(stream * stream, axis=1, keepdims=True)
    inv_std = lax.rsqrt(squares - row_mean * row_mean + norm_eps)
    normed = (stream - row_mean) * inv_std
    normed_low = (normed * gain_vec.astype(jnp.float32)).astype(jnp.bfloat16)
    return (normed, inv_std, normed_low)


def norm_backward(normed_grad, normed, inv_std, gain_vec):
    scaled = normed_grad * gain_vec.astype(jnp.float32)
    first_mean = jnp.mean(scaled, axis=1, keepdims=True)
    second_mean = jnp.mean(scaled * normed, axis=1, keepdims=True)
    stream_grad = inv_std * (scaled - first_mean - normed * second_mean)
    return (stream_grad, jnp.sum(normed_grad * normed, axis=0))


def rope_lanes(position):
    half = HEAD_DIM // 2
    lane = jnp.arange(LANES, dtype=jnp.int32)
    inv_freq = rope_base ** (-2.0 * (lane % half).astype(jnp.float32) / HEAD_DIM)
    angles = position.astype(jnp.float32)[:, None] * inv_freq[None, :]
    cos_tab, sin_tab = jnp.cos(angles), jnp.sin(angles)
    low_half = (lane < half)[None, :]
    high_half = ((lane >= half) & (lane < HEAD_DIM))[None, :]
    return (cos_tab, jnp.where(low_half, -sin_tab, 0.0), jnp.where(high_half, sin_tab, 0.0))


def mask_lanes(segment):
    lane = jnp.arange(LANES, dtype=jnp.int32)[None, :]
    used = (lane >= HEAD_DIM) & (lane < HEAD_DIM + 3)
    same = (segment[:, None] + HEAD_DIM) == lane
    query_side = jnp.where(used & ~same, masked_score, 0.0)
    key_side = jnp.where(same, 1.0, 0.0)
    ones = ((lane >= HEAD_DIM + 3) & (lane < HEAD_DIM + 6)).astype(jnp.float32)
    return (query_side.astype(jnp.bfloat16), (key_side + ones).astype(jnp.bfloat16))


def turn(u, cos_tab, low_tab, high_tab):
    half = HEAD_DIM // 2
    return (
        u * cos_tab + pltpu.roll(u, LANES - half, 1) * low_tab + pltpu.roll(u, half, 1) * high_tab
    )


def forward_kernel(
    rows, h1_ref, w_ref, cos_ref, low_ref, high_ref, fq_ref, fk_ref, qa_ref, ka_ref, va_ref, ctx_ref
):
    block = pl.program_id(1)
    total = h1_ref.shape[0]

    @pl.when(block == 0)
    def _():
        def part(i, carry):
            at = pl.ds(pl.multiple_of(i * rows, rows), rows)
            u = matmul(h1_ref[at, :], w_ref[0])
            tables = (cos_ref[at, :], low_ref[at, :], high_ref[at, :])
            lane = lax.broadcasted_iota(jnp.int32, (rows, LANES), 1)
            used = lane < HEAD_DIM
            q = turn(u[:, :LANES], *tables).astype(jnp.bfloat16).astype(jnp.float32)
            k = turn(u[:, LANES : 2 * LANES], *tables)
            v = u[:, 2 * LANES :]
            scale = HEAD_DIM**-0.5
            qa_ref[0, at, :] = jnp.where(used, q * scale, fq_ref[at, :].astype(jnp.float32)).astype(
                jnp.bfloat16
            )
            ka_ref[0, at, :] = jnp.where(used, k, fk_ref[at, :].astype(jnp.float32)).astype(
                jnp.bfloat16
            )
            ones = (lane < HEAD_DIM + 3).astype(jnp.float32)
            va_ref[0, at, :] = jnp.where(used, v, ones).astype(jnp.bfloat16)
            return carry

        lax.fori_loop(0, total // rows, part, 0)

    at = pl.ds(pl.multiple_of(block * rows, rows), rows)
    scores = times_transposed(qa_ref[0, at, :], ka_ref[0])
    peak = jnp.max(scores, axis=1, keepdims=True)
    exponent = jnp.exp(scores - peak).astype(jnp.bfloat16)
    summed = matmul(exponent, va_ref[0])
    totals = summed[:, HEAD_DIM : HEAD_DIM + 1]
    lane = lax.broadcasted_iota(jnp.int32, summed.shape, 1)
    ctx_ref[0] = jnp.where(lane < HEAD_DIM, summed / totals, peak + jnp.log(totals))


def attend_forward(h1, weights, tables, feats):
    total = h1.shape[0]
    heads = weights.shape[0]
    rows = 256
    whole = lambda shape: pl.BlockSpec(shape, lambda h, i: (0,) * len(shape))
    per_head = lambda shape: pl.BlockSpec((1, *shape), lambda h, i: (h, 0, 0))
    out = jax.ShapeDtypeStruct((heads, total, LANES), jnp.bfloat16)
    return pl.pallas_call(
        functools.partial(forward_kernel, rows),
        grid=(heads, total // rows),
        in_specs=[whole(h1.shape), per_head(weights.shape[1:])] + [whole((total, LANES))] * 5,
        out_specs=[per_head((total, LANES))] * 3
        + [pl.BlockSpec((1, rows, LANES), lambda h, i: (h, i, 0))],
        out_shape=[out, out, out, jax.ShapeDtypeStruct((heads, total, LANES), jnp.float32)],
        compiler_params=pltpu.CompilerParams(
            vmem_limit_bytes=VMEM_BYTES, dimension_semantics=("arbitrary", "arbitrary")
        ),
        cost_estimate=pl.CostEstimate(
            flops=heads * total * total * 1024, bytes_accessed=1 << 24, transcendentals=0
        ),
        name="attend_forward",
    )(h1, weights, *tables, *feats)


ROW_STEP = 4
COL_STEPS = (8, 12, 16, 18)
LAST_STEP = 23


def lane_sizes(grads):
    widths = [g.shape[1] // 2 for g in grads]
    padded = [-(-w // LANES) * LANES for w in widths]
    return widths, [sum(padded[:i]) for i in range(len(padded))], sum(padded)


def exchange_steps(
    step, grads, sums_ref, from_row, halves, from_col, pieces, from_packs, send_sems, recv_sems,
    pack_send, pack_recv,
):
    me_row, me_col, me_dp = (lax.axis_index(a) for a in ("row", "col", "dp"))
    peers = lax.axis_size("dp")
    half = grads[0].shape[0] // 2
    share = half // peers
    widths, starts, _ = lane_sizes(grads)
    mesh_ids = pl.DeviceIdType.MESH

    def row_copy(i):
        there = pl.ds(pl.multiple_of((1 - me_row) * half, half), half)
        return pltpu.make_async_remote_copy(
            src_ref=grads[i].at[there],
            dst_ref=from_row[i],
            send_sem=send_sems.at[i],
            recv_sem=recv_sems.at[i],
            device_id={"row": 1 - me_row},
            device_id_type=mesh_ids,
        )

    def col_copy(i):
        return pltpu.make_async_remote_copy(
            src_ref=halves[i].at[1 - me_col],
            dst_ref=from_col[i],
            send_sem=send_sems.at[4 + i],
            recv_sem=recv_sems.at[4 + i],
            device_id={"col": 1 - me_col},
            device_id_type=mesh_ids,
        )

    def pack_copy(i, d):
        peer = lax.rem(me_dp + d, peers)
        return pltpu.make_async_remote_copy(
            src_ref=pieces[i].at[peer],
            dst_ref=from_packs[i].at[d - 1],
            send_sem=pack_send.at[i, d - 1],
            recv_sem=pack_recv.at[i, d - 1],
            device_id={"dp": peer},
            device_id_type=mesh_ids,
        )

    def each_peer(f):
        def body(d, carry):
            f(d)
            return carry

        lax.fori_loop(1, peers, body, 0)

    @pl.when(step == 0)
    def _():
        barrier = pltpu.get_barrier_semaphore()
        for axis, me in (("row", me_row), ("col", me_col)):
            pl.semaphore_signal(barrier, inc=1, device_id={axis: 1 - me}, device_id_type=mesh_ids)
        each_peer(
            lambda d: pl.semaphore_signal(
                barrier,
                inc=1,
                device_id={"dp": lax.rem(me_dp + d, peers)},
                device_id_type=mesh_ids,
            )
        )
        pl.semaphore_wait(barrier, peers + 1)
        for i in range(4):
            row_copy(i).start()

    @pl.when(step == ROW_STEP)
    def _():
        for i in range(4):
            row_copy(i).wait_recv()
            here = pl.ds(pl.multiple_of(me_row * half, half), half)
            both = grads[i][here, :].astype(jnp.float32) + from_row[i][...].astype(jnp.float32)
            for c in range(2):
                halves[i][c] = both[:, c * widths[i] : (c + 1) * widths[i]].astype(jnp.bfloat16)
            col_copy(i).start()

    for i, at_step in enumerate(COL_STEPS):

        @pl.when(step == at_step)
        def _(i=i):
            col_copy(i).wait_recv()
            both = halves[i][me_col].astype(jnp.float32) + from_col[i][...].astype(jnp.float32)
            for p in range(peers):
                pieces[i][p] = both[p * share : (p + 1) * share].astype(jnp.bfloat16)
            each_peer(lambda d: pack_copy(i, d).start())

    @pl.when(step == LAST_STEP)
    def _():
        for i in range(4):
            sums = pieces[i][me_dp].astype(jnp.float32)

            def add(d, sums):
                pack_copy(i, d).wait_recv()
                return sums + from_packs[i][d - 1].astype(jnp.float32)

            sums = lax.fori_loop(1, peers, add, sums)
            sums_ref[:, starts[i] : starts[i] + widths[i]] = sums
            row_copy(i).wait_send()
            col_copy(i).wait_send()
            each_peer(lambda d: pack_copy(i, d).wait_send())


def backward_kernel(
    rows,
    qa_ref,
    ka_ref,
    va_ref,
    g_ref,
    ctx_ref,
    cos_ref,
    low_ref,
    high_ref,
    *rest,
):
    grads, (out_ref, sums_ref) = rest[:4], rest[4:6]
    qa_full, ga_full, dk_acc, dv_acc = rest[6:10]
    block = pl.program_id(1)
    last = pl.num_programs(1) - 1
    step = pl.program_id(0) * pl.num_programs(1) + block
    total = ka_ref.shape[1]
    exchange_steps(
        step, grads, sums_ref, rest[10:14], rest[14:18], rest[18:22], rest[22:26], rest[26:30], *rest[30:]
    )
    lane = lax.broadcasted_iota(jnp.int32, (rows, LANES), 1)
    used = lane < HEAD_DIM

    def with_parts(base, first, column):
        high = column.astype(jnp.bfloat16).astype(jnp.float32)
        middle = (column - high).astype(jnp.bfloat16).astype(jnp.float32)
        base = jnp.where(lane == first, high, base)
        base = jnp.where(lane == first + 1, middle, base)
        return jnp.where(lane == first + 2, column - high - middle, base).astype(jnp.bfloat16)

    @pl.when(block == 0)
    def _():
        def part(i, carry):
            here = pl.ds(pl.multiple_of(i * rows, rows), rows)
            g = g_ref[0, here, :].astype(jnp.float32)
            g = jnp.concatenate([g, jnp.zeros_like(g)], axis=1)
            ctx = ctx_ref[0, here, :]
            inner = jnp.sum(jnp.where(used, g * ctx, 0.0), axis=1, keepdims=True)
            ga_full[here, :] = with_parts(g, HEAD_DIM, -inner)
            qa_full[here, :] = with_parts(
                qa_ref[0, here, :].astype(jnp.float32),
                HEAD_DIM + 3,
                -ctx[:, HEAD_DIM : HEAD_DIM + 1],
            )
            return carry

        lax.fori_loop(0, total // rows, part, 0)

    at = pl.ds(pl.multiple_of(block * rows, rows), rows)
    qa = qa_full[at, :]
    ga = ga_full[at, :]
    probs = jnp.exp(times_transposed(ka_ref[0], qa))
    probs_low = probs.astype(jnp.bfloat16)
    dprobs = times_transposed(va_ref[0], ga)
    dscores = (probs * dprobs).astype(jnp.bfloat16)
    dv = matmul(probs_low, ga)
    dk = matmul(dscores, qa)

    @pl.when(block == 0)
    def _():
        dv_acc[...] = dv
        dk_acc[...] = dk

    @pl.when(block > 0)
    def _():
        dv_acc[...] += dv
        dk_acc[...] += dk

    dq = transposed_times(dscores, ka_ref[0]) * HEAD_DIM**-0.5

    def back(u, at):
        u = jnp.where(used, u, 0.0)
        return jnp.where(used, turn(u, cos_ref[at, :], -low_ref[at, :], -high_ref[at, :]), 0.0)

    out_ref[0, at, :LANES] = back(dq, at).astype(jnp.bfloat16)

    @pl.when(block == last)
    def _():
        def part(i, carry):
            here = pl.ds(pl.multiple_of(i * rows, rows), rows)
            out_ref[0, here, LANES : 2 * LANES] = back(dk_acc[here, :], here).astype(jnp.bfloat16)
            out_ref[0, here, 2 * LANES :] = jnp.where(used, dv_acc[here, :], 0.0).astype(
                jnp.bfloat16
            )
            return carry

        lax.fori_loop(0, total // rows, part, 0)


def attend_backward(qa, ka, va, head_grads, ctx, tables, grads, collective_id):
    heads, total, _ = qa.shape
    rows = total * heads // (LAST_STEP + 1)
    peers = lax.axis_size("dp")
    half = grads[0].shape[0] // 2
    share = half // peers
    widths, _, padded = lane_sizes(grads)
    low = lambda *shape: pltpu.VMEM(shape, jnp.bfloat16)
    whole = lambda shape: pl.BlockSpec(shape, lambda h, i: (0,) * len(shape))
    per_head = lambda shape: pl.BlockSpec((1, *shape), lambda h, i: (h, 0, 0))
    in_vmem = pl.BlockSpec(memory_space=pltpu.VMEM)
    return pl.pallas_call(
        functools.partial(backward_kernel, rows),
        grid=(heads, total // rows),
        in_specs=[per_head((total, LANES))] * 3
        + [per_head((total, HEAD_DIM)), per_head((total, LANES))]
        + [whole((total, LANES))] * 3
        + [in_vmem] * 4,
        out_specs=[per_head((total, 3 * LANES)), whole((share, padded))],
        out_shape=[
            jax.ShapeDtypeStruct((heads, total, 3 * LANES), jnp.bfloat16),
            jax.ShapeDtypeStruct((share, padded), jnp.float32),
        ],
        scratch_shapes=[low(total, LANES)] * 2
        + [pltpu.VMEM((total, LANES), jnp.float32)] * 2
        + [low(half, 2 * w) for w in widths]
        + [low(2, half, w) for w in widths]
        + [low(half, w) for w in widths]
        + [low(peers, share, w) for w in widths]
        + [low(peers - 1, share, w) for w in widths]
        + [pltpu.SemaphoreType.DMA((8,))] * 2
        + [pltpu.SemaphoreType.DMA((4, peers - 1))] * 2,
        compiler_params=pltpu.CompilerParams(
            vmem_limit_bytes=VMEM_BYTES,
            dimension_semantics=("arbitrary", "arbitrary"),
            collective_id=collective_id,
            has_side_effects=True,
        ),
        cost_estimate=pl.CostEstimate(
            flops=heads * total * total * 2560, bytes_accessed=1 << 24, transcendentals=0
        ),
        name="attend_backward",
    )(qa, ka, va, head_grads, ctx, *tables, *grads)


def pack_sum_kernel(peers, x_ref, out_ref, got, send_sems, recv_sems):
    me = lax.axis_index("dp")
    barrier = pltpu.get_barrier_semaphore()
    for d in range(1, peers):
        pl.semaphore_signal(
            barrier,
            inc=1,
            device_id={"dp": lax.rem(me + d, peers)},
            device_id_type=pl.DeviceIdType.MESH,
        )
    pl.semaphore_wait(barrier, peers - 1)
    copies = []
    for d in range(1, peers):
        peer = lax.rem(me + d, peers)
        copy = pltpu.make_async_remote_copy(
            src_ref=x_ref.at[peer],
            dst_ref=got.at[d - 1],
            send_sem=send_sems.at[d - 1],
            recv_sem=recv_sems.at[d - 1],
            device_id={"dp": peer},
            device_id_type=pl.DeviceIdType.MESH,
        )
        copy.start()
        copies.append(copy)
    out_ref[...] = x_ref[me].astype(jnp.float32)
    for d, copy in enumerate(copies):
        copy.wait_recv()
        out_ref[...] += got[d].astype(jnp.float32)
    for copy in copies:
        copy.wait_send()


def sum_over_packs(array, collective_id):
    peers = array.shape[0]
    vmem = pl.BlockSpec(memory_space=pltpu.VMEM)
    return pl.pallas_call(
        functools.partial(pack_sum_kernel, peers),
        in_specs=[vmem],
        out_specs=vmem,
        out_shape=jax.ShapeDtypeStruct(array.shape[1:], jnp.float32),
        scratch_shapes=[
            pltpu.VMEM((peers - 1, *array.shape[1:]), jnp.bfloat16),
            pltpu.SemaphoreType.DMA((peers - 1,)),
            pltpu.SemaphoreType.DMA((peers - 1,)),
        ],
        compiler_params=pltpu.CompilerParams(
            vmem_limit_bytes=VMEM_BYTES, collective_id=collective_id, has_side_effects=True
        ),
        name="sum_over_packs",
    )(array)


def swap_tokens_for_heads(values):
    quarter = values.shape[0]
    cut = values.reshape(quarter, 2, 2, -1).transpose(2, 1, 0, 3).reshape(4, quarter, -1)
    return lax.all_to_all(cut, ("row", "col"), split_axis=0, concat_axis=0, tiled=True).reshape(
        4 * quarter, -1
    )


def swap_heads_for_tokens(values):
    quarter = values.shape[0] // 4
    got = lax.all_to_all(
        values.reshape(4, quarter, -1), ("row", "col"), split_axis=0, concat_axis=0, tiled=True
    )
    return got.reshape(2, 2, quarter, -1).transpose(2, 1, 0, 3).reshape(quarter, -1)


def gather_quarters(values):
    return lax.all_gather(values, ("row", "col"), axis=0, tiled=True)


def whole_weight(weight, first, second):
    weight = lax.all_gather(weight, second, axis=1, tiled=True)
    return lax.all_gather(weight, first, axis=0, tiled=True)


def shards(
    layer_input,
    attn_gain,
    query_weight,
    key_weight,
    value_weight,
    out_weight,
    mlp_gain,
    act_weight,
    lin_weight,
    down_weight,
    seq_lengths,
    output_grad,
):
    bf16 = jnp.bfloat16
    stream = layer_input.astype(jnp.float32)
    quarter = stream.shape[0]
    total = quarter * 4
    segment, position = token_layout(seq_lengths[0], total)
    tables = rope_lanes(position)
    feats = mask_lanes(segment)
    normed_attn, inv_attn, low_attn = norm_forward(stream, attn_gain)

    stacked = jnp.stack((query_weight, key_weight, value_weight), axis=1)
    own = lax.all_to_all(stacked, "row", split_axis=2, concat_axis=0, tiled=True)
    own_heads = own.shape[2] // HEAD_DIM
    per_head = own.reshape(D, 3, own_heads, HEAD_DIM).transpose(2, 0, 1, 3)
    head_weights = jnp.pad(per_head, ((0, 0), (0, 0), (0, 0), (0, LANES - HEAD_DIM))).reshape(
        own_heads, D, 3 * LANES
    )

    h1 = gather_quarters(low_attn)
    qa, ka, va, ctx = attend_forward(h1, head_weights, tables, feats)
    context_heads = ctx[:, :, :HEAD_DIM]
    context_own = context_heads.astype(bf16).transpose(1, 0, 2).reshape(total, -1)

    out_whole = whole_weight(out_weight, "col", "row")
    act_whole = whole_weight(act_weight, "row", "col")
    lin_whole = whole_weight(lin_weight, "row", "col")
    down_whole = whole_weight(down_weight, "col", "row")

    context = swap_heads_for_tokens(context_own)
    middle = stream + matmul(context, out_whole)
    normed_mlp, inv_mlp, low_mlp = norm_forward(middle, mlp_gain)
    act = matmul(low_mlp, act_whole)
    lin = matmul(low_mlp, lin_whole)
    cdf = 0.5 * (1.0 + lax.erf(act * (0.5**0.5)))
    gelu = act * cdf
    hidden = (gelu * lin).astype(bf16)
    layer_output = (middle + matmul(hidden, down_whole)).astype(bf16)

    top_grad = output_grad.astype(jnp.float32)
    grad_down = transposed_times(output_grad, hidden).astype(bf16)
    hidden_grad = times_transposed(output_grad, down_whole)
    pdf = jnp.exp(-0.5 * act * act) * (0.5 / jnp.pi) ** 0.5
    act_grad = (hidden_grad * lin * (cdf + act * pdf)).astype(bf16)
    lin_grad = (hidden_grad * gelu).astype(bf16)
    grad_act = transposed_times(low_mlp, act_grad).astype(bf16)
    grad_lin = transposed_times(low_mlp, lin_grad).astype(bf16)
    mlp_norm_grad = times_transposed(act_grad, act_whole) + times_transposed(lin_grad, lin_whole)
    middle_back, gain_mlp_part = norm_backward(mlp_norm_grad, normed_mlp, inv_mlp, mlp_gain)
    middle_grad = top_grad + middle_back
    attn_grad = middle_grad.astype(bf16)
    grad_out = transposed_times(attn_grad, context).astype(bf16)
    context_grad = times_transposed(attn_grad, out_whole).astype(bf16)
    grad_own = swap_tokens_for_heads(context_grad)

    grad_heads = grad_own.reshape(total, own_heads, HEAD_DIM).transpose(1, 0, 2)
    late_grads = (grad_act, grad_lin, grad_down, grad_out)
    qkv_grad, late_sums = attend_backward(qa, ka, va, grad_heads, ctx, tables, late_grads, 1)

    norm_partial = lax.dot_general(
        qkv_grad,
        head_weights,
        (((0, 2), (0, 2)), ((), ())),
        preferred_element_type=jnp.float32,
    ).astype(bf16)
    pieces = lax.all_to_all(
        norm_partial.reshape(4, quarter, D), ("row", "col"), split_axis=0, concat_axis=0, tiled=True
    )
    attn_norm_grad = pieces.astype(jnp.float32).sum(axis=0)
    head_grads = lax.dot_general(
        h1, qkv_grad, (((0,), (1,)), ((), ())), preferred_element_type=jnp.float32
    ).astype(bf16)
    head_grads = head_grads.reshape(D, own_heads, 3, LANES)[..., :HEAD_DIM]
    head_grads = head_grads.transpose(0, 2, 1, 3).reshape(D, 3, own_heads * HEAD_DIM)
    attn_weight_grad = lax.all_to_all(head_grads, "row", split_axis=0, concat_axis=2, tiled=True)
    stream_back, gain_attn_part = norm_backward(attn_norm_grad, normed_attn, inv_attn, attn_gain)
    grad_input = middle_grad + stream_back

    peers = lax.axis_size("dp")
    half = D // 2
    mine = attn_weight_grad.reshape(peers, half // peers, -1)
    qkv_sums = sum_over_packs(mine, 0).reshape(-1, 3, half)
    widths, starts, _ = lane_sizes(late_grads)
    grad_act, grad_lin, grad_down, grad_out = (
        late_sums[:, a : a + w] for a, w in zip(starts, widths)
    )
    grad_down, grad_out = grad_down.T, grad_out.T
    devices = peers * 4
    gain_parts = jnp.stack((gain_attn_part, gain_mlp_part), axis=0).reshape(2, devices, -1)
    gains = (
        lax.all_to_all(
            gain_parts.swapaxes(0, 1).reshape(devices, -1),
            ("dp", "row", "col"),
            split_axis=0,
            concat_axis=0,
            tiled=True,
        )
        .sum(axis=0)
        .reshape(2, -1)
    )
    return (
        layer_output,
        grad_input,
        gains[0],
        qkv_sums[:, 0],
        qkv_sums[:, 1],
        qkv_sums[:, 2],
        grad_out,
        gains[1],
        grad_act,
        grad_lin,
        grad_down,
    )


def solution(mesh):
    in_specs = (
        P(("dp", "row", "col"), None),
        P(),
        P("row", "col"),
        P("row", "col"),
        P("row", "col"),
        P("col", "row"),
        P(),
        P("row", "col"),
        P("row", "col"),
        P("col", "row"),
        P("dp", None),
        P(("dp", "row", "col"), None),
    )
    out_specs = (
        P(("dp", "row", "col"), None),
        P(("dp", "row", "col"), None),
        P(("dp", "row", "col")),
        P(("row", "dp"), "col"),
        P(("row", "dp"), "col"),
        P(("row", "dp"), "col"),
        P("col", ("row", "dp")),
        P(("dp", "row", "col")),
        P(("row", "dp"), "col"),
        P(("row", "dp"), "col"),
        P("col", ("row", "dp")),
    )
    return jax.shard_map(shards, mesh=mesh, in_specs=in_specs, out_specs=out_specs, check_vma=False)
```

```python
import functools

import jax
import jax.numpy as jnp
from jax import lax
from jax.experimental import pallas as pl
from jax.experimental.pallas import tpu as pltpu
from jax.sharding import PartitionSpec as P

D = 768
HEADS = 12
HEAD_DIM = 64
LANES = 128

norm_eps = 1e-05
rope_base = 160000.0
masked_score = -1e30
VMEM_BYTES = 56 * 1024 * 1024


def matmul(left_side, right_side):
    return jnp.dot(left_side, right_side, preferred_element_type=jnp.float32)


def times_transposed(left_side, right_side):
    return lax.dot_general(
        left_side, right_side, (((1,), (1,)), ((), ())), preferred_element_type=jnp.float32
    )


def transposed_times(left_side, right_side):
    return lax.dot_general(
        left_side, right_side, (((0,), (0,)), ((), ())), preferred_element_type=jnp.float32
    )


def token_layout(lengths, slot_count):
    seq_ends = jnp.cumsum(lengths, dtype=jnp.int32)
    places = jnp.arange(slot_count, dtype=jnp.int32)
    passed = (places[:, None] >= seq_ends[None, :]).astype(jnp.int32)
    segment = jnp.sum(passed, axis=1, dtype=jnp.int32)
    position = places - jnp.sum(passed * lengths[None, :], axis=1, dtype=jnp.int32)
    return (segment, position)


def norm_forward(stream, gain_vec):
    row_mean = jnp.mean(stream, axis=1, keepdims=True)
    squares = jnp.mean(stream * stream, axis=1, keepdims=True)
    inv_std = lax.rsqrt(squares - row_mean * row_mean + norm_eps)
    normed = (stream - row_mean) * inv_std
    normed_low = (normed * gain_vec.astype(jnp.float32)).astype(jnp.bfloat16)
    return (normed, inv_std, normed_low)


def norm_backward(normed_grad, normed, inv_std, gain_vec):
    scaled = normed_grad * gain_vec.astype(jnp.float32)
    first_mean = jnp.mean(scaled, axis=1, keepdims=True)
    second_mean = jnp.mean(scaled * normed, axis=1, keepdims=True)
    stream_grad = inv_std * (scaled - first_mean - normed * second_mean)
    return (stream_grad, jnp.sum(normed_grad * normed, axis=0))


def rope_lanes(position):
    half = HEAD_DIM // 2
    lane = jnp.arange(LANES, dtype=jnp.int32)
    inv_freq = rope_base ** (-2.0 * (lane % half).astype(jnp.float32) / HEAD_DIM)
    angles = position.astype(jnp.float32)[:, None] * inv_freq[None, :]
    cos_tab, sin_tab = jnp.cos(angles), jnp.sin(angles)
    low_half = (lane < half)[None, :]
    high_half = ((lane >= half) & (lane < HEAD_DIM))[None, :]
    return (cos_tab, jnp.where(low_half, -sin_tab, 0.0), jnp.where(high_half, sin_tab, 0.0))


def mask_lanes(segment):
    lane = jnp.arange(LANES, dtype=jnp.int32)[None, :]
    used = (lane >= HEAD_DIM) & (lane < HEAD_DIM + 3)
    same = (segment[:, None] + HEAD_DIM) == lane
    query_side = jnp.where(used & ~same, masked_score, 0.0)
    key_side = jnp.where(same, 1.0, 0.0)
    ones = ((lane >= HEAD_DIM + 3) & (lane < HEAD_DIM + 6)).astype(jnp.float32)
    return (query_side.astype(jnp.bfloat16), (key_side + ones).astype(jnp.bfloat16))


def turn(u, cos_tab, low_tab, high_tab):
    half = HEAD_DIM // 2
    return (
        u * cos_tab + pltpu.roll(u, LANES - half, 1) * low_tab + pltpu.roll(u, half, 1) * high_tab
    )


def pair_barrier():
    me_row, me_col = lax.axis_index("row"), lax.axis_index("col")
    barrier = pltpu.get_barrier_semaphore()
    for axis, me in (("row", me_row), ("col", me_col)):
        pl.semaphore_signal(
            barrier, inc=1, device_id={axis: 1 - me}, device_id_type=pl.DeviceIdType.MESH
        )
    pl.semaphore_wait(barrier, 2)


def gather_kernel(chunks, x_ref, kept_ref, sent_ref, h1_ref, w_ref, sends, recvs):
    me_row, me_col = lax.axis_index("row"), lax.axis_index("col")
    quarter = x_ref.shape[0]
    rows = quarter // chunks

    def place(row, col, k):
        return pl.ds(pl.multiple_of((row * 2 + col) * quarter + k * rows, rows), rows)

    def copy(src, dst, n, axis, me):
        return pltpu.make_async_remote_copy(
            src_ref=src,
            dst_ref=dst,
            send_sem=sends.at[n],
            recv_sem=recvs.at[n],
            device_id={axis: 1 - me},
            device_id_type=pl.DeviceIdType.MESH,
        )

    pair_barrier()
    over_y, over_row, passed_on = [], [], []
    for k in range(chunks):
        own = x_ref.at[pl.ds(k * rows, rows)]
        there = h1_ref.at[place(me_row, me_col, k)]
        over_y.append(copy(own, there, k, "col", me_col))
        over_y[-1].start()
    weights = copy(sent_ref, w_ref.at[me_row], 3 * chunks, "row", me_row)
    weights.start()
    for k in range(chunks):
        own = x_ref.at[pl.ds(k * rows, rows)]
        there = h1_ref.at[place(me_row, me_col, k)]
        over_row.append(copy(own, there, chunks + k, "row", me_row))
        over_row[-1].start()
    h1_ref[pl.ds(pl.multiple_of((me_row * 2 + me_col) * quarter, quarter), quarter), :] = x_ref[...]
    w_ref[me_row] = kept_ref[...]
    for k in range(chunks):
        over_y[k].wait_recv()
        arrived = h1_ref.at[place(me_row, 1 - me_col, k)]
        passed_on.append(copy(arrived, arrived, 2 * chunks + k, "row", me_row))
        passed_on[-1].start()
    for one in over_row + passed_on + [weights]:
        one.wait_recv()
    for one in over_y + over_row + passed_on + [weights]:
        one.wait_send()


def gather_rows(rows_low, kept, sent, collective_id):
    chunks = 4
    vmem = pl.BlockSpec(memory_space=pltpu.VMEM)
    return pl.pallas_call(
        functools.partial(gather_kernel, chunks),
        in_specs=[vmem] * 3,
        out_specs=[vmem] * 2,
        out_shape=[
            jax.ShapeDtypeStruct((4 * rows_low.shape[0], rows_low.shape[1]), jnp.bfloat16),
            jax.ShapeDtypeStruct((2, *kept.shape), jnp.bfloat16),
        ],
        scratch_shapes=[pltpu.SemaphoreType.DMA((3 * chunks + 1,))] * 2,
        compiler_params=pltpu.CompilerParams(
            vmem_limit_bytes=VMEM_BYTES, collective_id=collective_id, has_side_effects=True
        ),
        name="gather_rows",
    )(rows_low, kept, sent)


LAST_STEP = 23
PASS_STEP = 20


def gather_steps(step, blocks, wholes, local_sems, sends, recvs):
    me_row, me_col = lax.axis_index("row"), lax.axis_index("col")
    count = len(blocks)

    def place(i, row, col):
        first, second = (row, col) if i < 2 else (col, row)
        length = blocks[i].shape[0]
        return wholes[i].at[second, pl.ds(pl.multiple_of(first * length, length), length)]

    def copy(src, dst, n, axis, me):
        return pltpu.make_async_remote_copy(
            src_ref=src,
            dst_ref=dst,
            send_sem=sends.at[n],
            recv_sem=recvs.at[n],
            device_id={axis: 1 - me},
            device_id_type=pl.DeviceIdType.MESH,
        )

    def over_y(i):
        return copy(blocks[i], place(i, me_row, me_col), i, "col", me_col)

    def over_row(i):
        return copy(blocks[i], place(i, me_row, me_col), count + i, "row", me_row)

    def passed_on(i):
        arrived = place(i, me_row, 1 - me_col)
        return copy(arrived, arrived, 2 * count + i, "row", me_row)

    def local(i):
        return pltpu.make_async_copy(blocks[i], place(i, me_row, me_col), local_sems.at[i])

    @pl.when(step == 0)
    def _():
        pair_barrier()
        for i in range(count):
            over_y(i).start()
        for i in range(count):
            over_row(i).start()
            local(i).start()

    @pl.when(step == PASS_STEP)
    def _():
        for i in range(count):
            over_y(i).wait_recv()
            passed_on(i).start()

    @pl.when(step == LAST_STEP)
    def _():
        for i in range(count):
            over_row(i).wait_recv()
            passed_on(i).wait_recv()
            local(i).wait()
            over_y(i).wait_send()
            over_row(i).wait_send()
            passed_on(i).wait_send()


def forward_kernel(
    rows, h1_ref, w_ref, cos_ref, low_ref, high_ref, fq_ref, fk_ref, *rest
):
    blocks, (qa_ref, ka_ref, va_ref, ctx_ref), wholes = rest[:4], rest[4:8], rest[8:12]
    block = pl.program_id(1)
    total = h1_ref.shape[0]
    gather_steps(pl.program_id(0) * pl.num_programs(1) + block, blocks, wholes, *rest[12:])

    @pl.when(block == 0)
    def _():
        def part(i, carry):
            at = pl.ds(pl.multiple_of(i * rows, rows), rows)
            u = matmul(h1_ref[at, :], w_ref[0])
            tables = (cos_ref[at, :], low_ref[at, :], high_ref[at, :])
            lane = lax.broadcasted_iota(jnp.int32, (rows, LANES), 1)
            used = lane < HEAD_DIM
            q = turn(u[:, :LANES], *tables).astype(jnp.bfloat16).astype(jnp.float32)
            k = turn(u[:, LANES : 2 * LANES], *tables)
            v = u[:, 2 * LANES :]
            scale = HEAD_DIM**-0.5
            qa_ref[0, at, :] = jnp.where(used, q * scale, fq_ref[at, :].astype(jnp.float32)).astype(
                jnp.bfloat16
            )
            ka_ref[0, at, :] = jnp.where(used, k, fk_ref[at, :].astype(jnp.float32)).astype(
                jnp.bfloat16
            )
            ones = (lane < HEAD_DIM + 3).astype(jnp.float32)
            va_ref[0, at, :] = jnp.where(used, v, ones).astype(jnp.bfloat16)
            return carry

        lax.fori_loop(0, total // rows, part, 0)

    at = pl.ds(pl.multiple_of(block * rows, rows), rows)
    scores = times_transposed(qa_ref[0, at, :], ka_ref[0])
    peak = jnp.max(scores, axis=1, keepdims=True)
    exponent = jnp.exp(scores - peak).astype(jnp.bfloat16)
    summed = matmul(exponent, va_ref[0])
    totals = summed[:, HEAD_DIM : HEAD_DIM + 1]
    lane = lax.broadcasted_iota(jnp.int32, summed.shape, 1)
    ctx_ref[0] = jnp.where(lane < HEAD_DIM, summed / totals, peak + jnp.log(totals))


def attend_forward(h1, weights, tables, feats, blocks, collective_id):
    total = h1.shape[0]
    heads = weights.shape[0]
    rows = total * heads // (LAST_STEP + 1)
    anywhere = pl.BlockSpec(memory_space=pl.ANY)
    whole = lambda shape: pl.BlockSpec(shape, lambda h, i: (0,) * len(shape))
    per_head = lambda shape: pl.BlockSpec((1, *shape), lambda h, i: (h, 0, 0))
    out = jax.ShapeDtypeStruct((heads, total, LANES), jnp.bfloat16)
    return pl.pallas_call(
        functools.partial(forward_kernel, rows),
        grid=(heads, total // rows),
        in_specs=[whole(h1.shape), per_head(weights.shape[1:])]
        + [whole((total, LANES))] * 5
        + [anywhere] * 4,
        out_specs=[per_head((total, LANES))] * 3
        + [pl.BlockSpec((1, rows, LANES), lambda h, i: (h, i, 0))]
        + [anywhere] * 4,
        out_shape=[out, out, out, jax.ShapeDtypeStruct((heads, total, LANES), jnp.float32)]
        + [jax.ShapeDtypeStruct((2, 2 * b.shape[0], b.shape[1]), jnp.bfloat16) for b in blocks],
        scratch_shapes=[pltpu.SemaphoreType.DMA((n,)) for n in (4, 12, 12)],
        compiler_params=pltpu.CompilerParams(
            vmem_limit_bytes=VMEM_BYTES,
            dimension_semantics=("arbitrary", "arbitrary"),
            collective_id=collective_id,
            has_side_effects=True,
        ),
        cost_estimate=pl.CostEstimate(
            flops=heads * total * total * 1024, bytes_accessed=1 << 24, transcendentals=0
        ),
        name="attend_forward",
    )(h1, weights, *tables, *feats, *blocks)


ROW_STEP = 4
COL_STEPS = (8, 12, 16, 18)


def lane_sizes(grads):
    widths = [g.shape[1] // 2 for g in grads]
    padded = [-(-w // LANES) * LANES for w in widths]
    return widths, [sum(padded[:i]) for i in range(len(padded))], sum(padded)


def exchange_steps(
    step, grads, sums_ref, from_row, halves, from_col, pieces, from_packs, send_sems, recv_sems,
    pack_send, pack_recv,
):
    me_row, me_col, me_dp = (lax.axis_index(a) for a in ("row", "col", "dp"))
    peers = lax.axis_size("dp")
    half = grads[0].shape[0] // 2
    share = half // peers
    widths, starts, _ = lane_sizes(grads)
    mesh_ids = pl.DeviceIdType.MESH

    def row_copy(i):
        there = pl.ds(pl.multiple_of((1 - me_row) * half, half), half)
        return pltpu.make_async_remote_copy(
            src_ref=grads[i].at[there],
            dst_ref=from_row[i],
            send_sem=send_sems.at[i],
            recv_sem=recv_sems.at[i],
            device_id={"row": 1 - me_row},
            device_id_type=mesh_ids,
        )

    def col_copy(i):
        return pltpu.make_async_remote_copy(
            src_ref=halves[i].at[1 - me_col],
            dst_ref=from_col[i],
            send_sem=send_sems.at[4 + i],
            recv_sem=recv_sems.at[4 + i],
            device_id={"col": 1 - me_col},
            device_id_type=mesh_ids,
        )

    def pack_copy(i, d):
        peer = lax.rem(me_dp + d, peers)
        return pltpu.make_async_remote_copy(
            src_ref=pieces[i].at[peer],
            dst_ref=from_packs[i].at[d - 1],
            send_sem=pack_send.at[i, d - 1],
            recv_sem=pack_recv.at[i, d - 1],
            device_id={"dp": peer},
            device_id_type=mesh_ids,
        )

    def each_peer(f):
        def body(d, carry):
            f(d)
            return carry

        lax.fori_loop(1, peers, body, 0)

    @pl.when(step == 0)
    def _():
        barrier = pltpu.get_barrier_semaphore()
        for axis, me in (("row", me_row), ("col", me_col)):
            pl.semaphore_signal(barrier, inc=1, device_id={axis: 1 - me}, device_id_type=mesh_ids)
        each_peer(
            lambda d: pl.semaphore_signal(
                barrier,
                inc=1,
                device_id={"dp": lax.rem(me_dp + d, peers)},
                device_id_type=mesh_ids,
            )
        )
        pl.semaphore_wait(barrier, peers + 1)
        for i in range(4):
            row_copy(i).start()

    @pl.when(step == ROW_STEP)
    def _():
        for i in range(4):
            row_copy(i).wait_recv()
            here = pl.ds(pl.multiple_of(me_row * half, half), half)
            both = grads[i][here, :].astype(jnp.float32) + from_row[i][...].astype(jnp.float32)
            for c in range(2):
                halves[i][c] = both[:, c * widths[i] : (c + 1) * widths[i]].astype(jnp.bfloat16)
            col_copy(i).start()

    for i, at_step in enumerate(COL_STEPS):

        @pl.when(step == at_step)
        def _(i=i):
            col_copy(i).wait_recv()
            both = halves[i][me_col].astype(jnp.float32) + from_col[i][...].astype(jnp.float32)
            for p in range(peers):
                pieces[i][p] = both[p * share : (p + 1) * share].astype(jnp.bfloat16)
            each_peer(lambda d: pack_copy(i, d).start())

    @pl.when(step == LAST_STEP)
    def _():
        for i in range(4):
            sums = pieces[i][me_dp].astype(jnp.float32)

            def add(d, sums):
                pack_copy(i, d).wait_recv()
                return sums + from_packs[i][d - 1].astype(jnp.float32)

            sums = lax.fori_loop(1, peers, add, sums)
            sums_ref[:, starts[i] : starts[i] + widths[i]] = sums
            row_copy(i).wait_send()
            col_copy(i).wait_send()
            each_peer(lambda d: pack_copy(i, d).wait_send())


def backward_kernel(
    rows,
    qa_ref,
    ka_ref,
    va_ref,
    g_ref,
    ctx_ref,
    cos_ref,
    low_ref,
    high_ref,
    *rest,
):
    grads, (out_ref, sums_ref) = rest[:4], rest[4:6]
    qa_full, ga_full, dk_acc, dv_acc = rest[6:10]
    block = pl.program_id(1)
    last = pl.num_programs(1) - 1
    step = pl.program_id(0) * pl.num_programs(1) + block
    total = ka_ref.shape[1]
    exchange_steps(
        step, grads, sums_ref, rest[10:14], rest[14:18], rest[18:22], rest[22:26], rest[26:30], *rest[30:]
    )
    lane = lax.broadcasted_iota(jnp.int32, (rows, LANES), 1)
    used = lane < HEAD_DIM

    def with_parts(base, first, column):
        high = column.astype(jnp.bfloat16).astype(jnp.float32)
        middle = (column - high).astype(jnp.bfloat16).astype(jnp.float32)
        base = jnp.where(lane == first, high, base)
        base = jnp.where(lane == first + 1, middle, base)
        return jnp.where(lane == first + 2, column - high - middle, base).astype(jnp.bfloat16)

    @pl.when(block == 0)
    def _():
        def part(i, carry):
            here = pl.ds(pl.multiple_of(i * rows, rows), rows)
            g = g_ref[0, here, :].astype(jnp.float32)
            g = jnp.concatenate([g, jnp.zeros_like(g)], axis=1)
            ctx = ctx_ref[0, here, :]
            inner = jnp.sum(jnp.where(used, g * ctx, 0.0), axis=1, keepdims=True)
            ga_full[here, :] = with_parts(g, HEAD_DIM, -inner)
            qa_full[here, :] = with_parts(
                qa_ref[0, here, :].astype(jnp.float32),
                HEAD_DIM + 3,
                -ctx[:, HEAD_DIM : HEAD_DIM + 1],
            )
            return carry

        lax.fori_loop(0, total // rows, part, 0)

    at = pl.ds(pl.multiple_of(block * rows, rows), rows)
    qa = qa_full[at, :]
    ga = ga_full[at, :]
    probs = jnp.exp(times_transposed(ka_ref[0], qa))
    probs_low = probs.astype(jnp.bfloat16)
    dprobs = times_transposed(va_ref[0], ga)
    dscores = (probs * dprobs).astype(jnp.bfloat16)
    dv = matmul(probs_low, ga)
    dk = matmul(dscores, qa)

    @pl.when(block == 0)
    def _():
        dv_acc[...] = dv
        dk_acc[...] = dk

    @pl.when(block > 0)
    def _():
        dv_acc[...] += dv
        dk_acc[...] += dk

    dq = transposed_times(dscores, ka_ref[0]) * HEAD_DIM**-0.5

    def back(u, at):
        u = jnp.where(used, u, 0.0)
        return jnp.where(used, turn(u, cos_ref[at, :], -low_ref[at, :], -high_ref[at, :]), 0.0)

    out_ref[0, at, :LANES] = back(dq, at).astype(jnp.bfloat16)

    @pl.when(block == last)
    def _():
        def part(i, carry):
            here = pl.ds(pl.multiple_of(i * rows, rows), rows)
            out_ref[0, here, LANES : 2 * LANES] = back(dk_acc[here, :], here).astype(jnp.bfloat16)
            out_ref[0, here, 2 * LANES :] = jnp.where(used, dv_acc[here, :], 0.0).astype(
                jnp.bfloat16
            )
            return carry

        lax.fori_loop(0, total // rows, part, 0)


def attend_backward(qa, ka, va, head_grads, ctx, tables, grads, collective_id):
    heads, total, _ = qa.shape
    rows = total * heads // (LAST_STEP + 1)
    peers = lax.axis_size("dp")
    half = grads[0].shape[0] // 2
    share = half // peers
    widths, _, padded = lane_sizes(grads)
    low = lambda *shape: pltpu.VMEM(shape, jnp.bfloat16)
    whole = lambda shape: pl.BlockSpec(shape, lambda h, i: (0,) * len(shape))
    per_head = lambda shape: pl.BlockSpec((1, *shape), lambda h, i: (h, 0, 0))
    in_vmem = pl.BlockSpec(memory_space=pltpu.VMEM)
    return pl.pallas_call(
        functools.partial(backward_kernel, rows),
        grid=(heads, total // rows),
        in_specs=[per_head((total, LANES))] * 3
        + [per_head((total, HEAD_DIM)), per_head((total, LANES))]
        + [whole((total, LANES))] * 3
        + [in_vmem] * 4,
        out_specs=[per_head((total, 3 * LANES)), whole((share, padded))],
        out_shape=[
            jax.ShapeDtypeStruct((heads, total, 3 * LANES), jnp.bfloat16),
            jax.ShapeDtypeStruct((share, padded), jnp.float32),
        ],
        scratch_shapes=[low(total, LANES)] * 2
        + [pltpu.VMEM((total, LANES), jnp.float32)] * 2
        + [low(half, 2 * w) for w in widths]
        + [low(2, half, w) for w in widths]
        + [low(half, w) for w in widths]
        + [low(peers, share, w) for w in widths]
        + [low(peers - 1, share, w) for w in widths]
        + [pltpu.SemaphoreType.DMA((8,))] * 2
        + [pltpu.SemaphoreType.DMA((4, peers - 1))] * 2,
        compiler_params=pltpu.CompilerParams(
            vmem_limit_bytes=VMEM_BYTES,
            dimension_semantics=("arbitrary", "arbitrary"),
            collective_id=collective_id,
            has_side_effects=True,
        ),
        cost_estimate=pl.CostEstimate(
            flops=heads * total * total * 2560, bytes_accessed=1 << 24, transcendentals=0
        ),
        name="attend_backward",
    )(qa, ka, va, head_grads, ctx, *tables, *grads)


def pack_sum_kernel(peers, x_ref, out_ref, got, send_sems, recv_sems):
    me = lax.axis_index("dp")
    barrier = pltpu.get_barrier_semaphore()
    for d in range(1, peers):
        pl.semaphore_signal(
            barrier,
            inc=1,
            device_id={"dp": lax.rem(me + d, peers)},
            device_id_type=pl.DeviceIdType.MESH,
        )
    pl.semaphore_wait(barrier, peers - 1)
    copies = []
    for d in range(1, peers):
        peer = lax.rem(me + d, peers)
        copy = pltpu.make_async_remote_copy(
            src_ref=x_ref.at[peer],
            dst_ref=got.at[d - 1],
            send_sem=send_sems.at[d - 1],
            recv_sem=recv_sems.at[d - 1],
            device_id={"dp": peer},
            device_id_type=pl.DeviceIdType.MESH,
        )
        copy.start()
        copies.append(copy)
    out_ref[...] = x_ref[me].astype(jnp.float32)
    for d, copy in enumerate(copies):
        copy.wait_recv()
        out_ref[...] += got[d].astype(jnp.float32)
    for copy in copies:
        copy.wait_send()


def sum_over_packs(array, collective_id):
    peers = array.shape[0]
    vmem = pl.BlockSpec(memory_space=pltpu.VMEM)
    return pl.pallas_call(
        functools.partial(pack_sum_kernel, peers),
        in_specs=[vmem],
        out_specs=vmem,
        out_shape=jax.ShapeDtypeStruct(array.shape[1:], jnp.float32),
        scratch_shapes=[
            pltpu.VMEM((peers - 1, *array.shape[1:]), jnp.bfloat16),
            pltpu.SemaphoreType.DMA((peers - 1,)),
            pltpu.SemaphoreType.DMA((peers - 1,)),
        ],
        compiler_params=pltpu.CompilerParams(
            vmem_limit_bytes=VMEM_BYTES, collective_id=collective_id, has_side_effects=True
        ),
        name="sum_over_packs",
    )(array)


def swap_tokens_for_heads(values):
    quarter = values.shape[0]
    cut = values.reshape(quarter, 2, 2, -1).transpose(2, 1, 0, 3).reshape(4, quarter, -1)
    return lax.all_to_all(cut, ("row", "col"), split_axis=0, concat_axis=0, tiled=True).reshape(
        4 * quarter, -1
    )


def swap_heads_for_tokens(values):
    quarter = values.shape[0] // 4
    got = lax.all_to_all(
        values.reshape(4, quarter, -1), ("row", "col"), split_axis=0, concat_axis=0, tiled=True
    )
    return got.reshape(2, 2, quarter, -1).transpose(2, 1, 0, 3).reshape(quarter, -1)


def shards(
    layer_input,
    attn_gain,
    query_weight,
    key_weight,
    value_weight,
    out_weight,
    mlp_gain,
    act_weight,
    lin_weight,
    down_weight,
    seq_lengths,
    output_grad,
):
    bf16 = jnp.bfloat16
    stream = layer_input.astype(jnp.float32)
    quarter = stream.shape[0]
    total = quarter * 4
    segment, position = token_layout(seq_lengths[0], total)
    tables = rope_lanes(position)
    feats = mask_lanes(segment)
    normed_attn, inv_attn, low_attn = norm_forward(stream, attn_gain)

    half = D // 2
    stacked = jnp.concatenate((query_weight, key_weight, value_weight), axis=1)
    cut = stacked.reshape(half, 3, 2, -1).transpose(2, 0, 1, 3).reshape(2, half, -1)
    me_row = lax.axis_index("row")
    kept = lax.dynamic_index_in_dim(cut, me_row, 0, keepdims=False)
    sent = lax.dynamic_index_in_dim(cut, 1 - me_row, 0, keepdims=False)
    h1, own = gather_rows(low_attn, kept, sent, 2)
    own_heads = kept.shape[1] // (3 * HEAD_DIM)
    per_head = own.reshape(D, 3, own_heads, HEAD_DIM).transpose(2, 0, 1, 3)
    head_weights = jnp.pad(per_head, ((0, 0), (0, 0), (0, 0), (0, LANES - HEAD_DIM))).reshape(
        own_heads, D, 3 * LANES
    )

    qa, ka, va, ctx, *wholes = attend_forward(
        h1, head_weights, tables, feats, (act_weight, lin_weight, out_weight, down_weight), 3
    )
    context_heads = ctx[:, :, :HEAD_DIM]
    context_own = context_heads.astype(bf16).transpose(1, 0, 2).reshape(total, -1)
    act_whole, lin_whole, out_whole, down_whole = (
        jnp.concatenate((w[0], w[1]), axis=1) for w in wholes
    )

    context = swap_heads_for_tokens(context_own)
    middle = stream + matmul(context, out_whole)
    normed_mlp, inv_mlp, low_mlp = norm_forward(middle, mlp_gain)
    act = matmul(low_mlp, act_whole)
    lin = matmul(low_mlp, lin_whole)
    cdf = 0.5 * (1.0 + lax.erf(act * (0.5**0.5)))
    gelu = act * cdf
    hidden = (gelu * lin).astype(bf16)
    layer_output = (middle + matmul(hidden, down_whole)).astype(bf16)

    top_grad = output_grad.astype(jnp.float32)
    grad_down = transposed_times(output_grad, hidden).astype(bf16)
    hidden_grad = times_transposed(output_grad, down_whole)
    pdf = jnp.exp(-0.5 * act * act) * (0.5 / jnp.pi) ** 0.5
    act_grad = (hidden_grad * lin * (cdf + act * pdf)).astype(bf16)
    lin_grad = (hidden_grad * gelu).astype(bf16)
    grad_act = transposed_times(low_mlp, act_grad).astype(bf16)
    grad_lin = transposed_times(low_mlp, lin_grad).astype(bf16)
    mlp_norm_grad = times_transposed(act_grad, act_whole) + times_transposed(lin_grad, lin_whole)
    middle_back, gain_mlp_part = norm_backward(mlp_norm_grad, normed_mlp, inv_mlp, mlp_gain)
    middle_grad = top_grad + middle_back
    attn_grad = middle_grad.astype(bf16)
    grad_out = transposed_times(attn_grad, context).astype(bf16)
    context_grad = times_transposed(attn_grad, out_whole).astype(bf16)
    grad_own = swap_tokens_for_heads(context_grad)

    grad_heads = grad_own.reshape(total, own_heads, HEAD_DIM).transpose(1, 0, 2)
    late_grads = (grad_act, grad_lin, grad_down, grad_out)
    qkv_grad, late_sums = attend_backward(qa, ka, va, grad_heads, ctx, tables, late_grads, 1)

    norm_partial = lax.dot_general(
        qkv_grad,
        head_weights,
        (((0, 2), (0, 2)), ((), ())),
        preferred_element_type=jnp.float32,
    ).astype(bf16)
    pieces = lax.all_to_all(
        norm_partial.reshape(4, quarter, D), ("row", "col"), split_axis=0, concat_axis=0, tiled=True
    )
    attn_norm_grad = pieces.astype(jnp.float32).sum(axis=0)
    head_grads = lax.dot_general(
        h1, qkv_grad, (((0,), (1,)), ((), ())), preferred_element_type=jnp.float32
    ).astype(bf16)
    head_grads = head_grads.reshape(D, own_heads, 3, LANES)[..., :HEAD_DIM]
    head_grads = head_grads.transpose(0, 2, 1, 3).reshape(D, 3, own_heads * HEAD_DIM)
    attn_weight_grad = lax.all_to_all(head_grads, "row", split_axis=0, concat_axis=2, tiled=True)
    stream_back, gain_attn_part = norm_backward(attn_norm_grad, normed_attn, inv_attn, attn_gain)
    grad_input = middle_grad + stream_back

    peers = lax.axis_size("dp")
    mine = attn_weight_grad.reshape(peers, half // peers, -1)
    qkv_sums = sum_over_packs(mine, 0).reshape(-1, 3, half)
    widths, starts, _ = lane_sizes(late_grads)
    grad_act, grad_lin, grad_down, grad_out = (
        late_sums[:, a : a + w] for a, w in zip(starts, widths)
    )
    grad_down, grad_out = grad_down.T, grad_out.T
    devices = peers * 4
    gain_parts = jnp.stack((gain_attn_part, gain_mlp_part), axis=0).reshape(2, devices, -1)
    gains = (
        lax.all_to_all(
            gain_parts.swapaxes(0, 1).reshape(devices, -1),
            ("dp", "row", "col"),
            split_axis=0,
            concat_axis=0,
            tiled=True,
        )
        .sum(axis=0)
        .reshape(2, -1)
    )
    return (
        layer_output,
        grad_input,
        gains[0],
        qkv_sums[:, 0],
        qkv_sums[:, 1],
        qkv_sums[:, 2],
        grad_out,
        gains[1],
        grad_act,
        grad_lin,
        grad_down,
    )


def solution(mesh):
    in_specs = (
        P(("dp", "row", "col"), None),
        P(),
        P("row", "col"),
        P("row", "col"),
        P("row", "col"),
        P("col", "row"),
        P(),
        P("row", "col"),
        P("row", "col"),
        P("col", "row"),
        P("dp", None),
        P(("dp", "row", "col"), None),
    )
    out_specs = (
        P(("dp", "row", "col"), None),
        P(("dp", "row", "col"), None),
        P(("dp", "row", "col")),
        P(("row", "dp"), "col"),
        P(("row", "dp"), "col"),
        P(("row", "dp"), "col"),
        P("col", ("row", "dp")),
        P(("dp", "row", "col")),
        P(("row", "dp"), "col"),
        P(("row", "dp"), "col"),
        P("col", ("row", "dp")),
    )
    return jax.shard_map(shards, mesh=mesh, in_specs=in_specs, out_specs=out_specs, check_vma=False)
```
